32 devices in a mesh: seq: 16 (over z, y, core), tp: 2 (over x).
Axes of the slice: x: 2, y: 2, z: 4, core: 2. Of those that a mesh axis runs over, the one named last changes fastest.
Arguments:
- queries: bfloat16 [4096, 8192], P('seq', 'tp'), may hold values from -12 to 12
- kv_rows: bfloat16 [4096, 2048], P('seq', 'tp'), may hold values from -6 to 6
- vertical: int32 [64, 8], replicated, may hold values from 0 to 63, as said below
- slash: int32 [64, 8], replicated, may hold values from 0 to 11, as said below
Outputs:
- attended: bfloat16 [4096, 8192], P(('seq', 'tp'))
The draws below stay inside these ranges and needn't reach their ends.
Inputs may be any that keep to these rules, and one draw needn't show every extreme that they name: `vertical`: each row lists 8 distinct blocks in rising order and includes block 0 and block 63. The heads that share one key-value head list together exactly 12 distinct blocks. `slash`: each row lists 8 distinct offsets in rising order, the first 0 and the last 11.
All inputs are finite; a program needn't handle non-finite values.
Results may differ from the reference program's by a relative error of at most 0.0045.
Values may be sent and summed in bfloat16 or wider, within the bound.
No kernel may reach another device: no remote copies, remote signals or barrier semaphores. Data moves between devices by JAX's collectives and lax.ppermute only.
A program may use at most 64 MiB of HBM per device.

```python
import jax
import jax.numpy as jnp
from jax import lax

HEADS = 64
KVH = 8
HEAD_SIZE = 128
BLK = 64
NSL = 8
SEQ = 4096
NB = 64
BLOCKS_PER_INDEX = 4
SMAX = 11
VERTICAL_COUNT = 8
GV = 12
N_SEQ = 16


def draw_queries(key, part):
    inner = jax.random.fold_in(key, 1)
    base = jax.random.truncated_normal(inner, -6.0, 6.0, (SEQ, HEADS, HEAD_SIZE), jnp.float32)
    return base.reshape(SEQ, HEADS * HEAD_SIZE).astype(jnp.bfloat16)


def draw_kv_rows(key, part):
    inner = jax.random.fold_in(key, 2)
    base = jax.random.truncated_normal(inner, -6.0, 6.0, (SEQ, KVH, 2, HEAD_SIZE), jnp.float32)
    return base.reshape(SEQ, KVH * 2 * HEAD_SIZE).astype(jnp.bfloat16)


def draw_vertical(key, part):
    group = HEADS // KVH
    middle_count = GV - 2
    gkeys = jax.random.split(jax.random.fold_in(key, 3), KVH)
    picks = jax.vmap(lambda sub: jax.random.permutation(sub, NB - 2))(gkeys)
    middle = jnp.sort(picks[:, :middle_count].astype(jnp.int32) + 1, axis=1)
    okeys = jax.random.split(jax.random.fold_in(key, 4), KVH)
    orders = jax.vmap(lambda sub: jax.random.permutation(sub, middle_count))(okeys).astype(jnp.int32)
    heads = jnp.arange(HEADS, dtype=jnp.int32)
    owner = heads // group
    member = heads % group
    starts = member * middle_count // group
    steps = jnp.arange(VERTICAL_COUNT - 2, dtype=jnp.int32)
    places = (starts[:, None] + steps[None, :]) % middle_count
    slots = jnp.take_along_axis(orders[owner], places, axis=1)
    taken = jnp.take_along_axis(middle[owner], slots, axis=1)
    firsts = jnp.zeros((HEADS, 1), jnp.int32)
    lasts = jnp.full((HEADS, 1), NB - 1, jnp.int32)
    return jnp.sort(jnp.concatenate([firsts, taken, lasts], axis=1), axis=1).astype(jnp.int32)


def draw_slash(key, part):
    subkeys = jax.random.split(jax.random.fold_in(key, 5), HEADS)
    shuffled = jax.vmap(lambda sub: jax.random.permutation(sub, SMAX - 1))(subkeys) + 1
    firsts = jnp.zeros((HEADS, 1), jnp.int32)
    lasts = jnp.full((HEADS, 1), SMAX, jnp.int32)
    rows = jnp.concatenate([firsts, shuffled[:, :NSL - 2].astype(jnp.int32), lasts], axis=1)
    return jnp.sort(rows, axis=1).astype(jnp.int32)


def setup_inputs(seed: int = 0) -> dict:
    splits = jax.random.split(jax.random.key(seed), 5)
    return {
        "queries": draw_queries(jax.random.fold_in(splits[4], 71), 0),
        "kv_rows": draw_kv_rows(jax.random.fold_in(splits[4], 71), 0),
        "vertical": draw_vertical(jax.random.fold_in(splits[4], 71), 0),
        "slash": draw_slash(jax.random.fold_in(splits[4], 71), 0),
    }


def key_mask(bids, vertical_row, srow):
    dist = bids[:, None] - vertical_row[None, :]
    hit = jnp.any(dist[:, :, None] == srow[None, None, :], axis=2)
    live_v = jnp.logical_and(dist >= 0, jnp.logical_not(hit))
    live_s = (bids[:, None] - srow[None, :]) >= 0
    live = jnp.concatenate([live_v, live_s], axis=1)
    diag = jnp.concatenate([jnp.zeros(vertical_row.shape, bool), srow == 0])
    rows = jnp.arange(BLK, dtype=jnp.int32)
    lower = rows[None, :] <= rows[:, None]
    return live[:, None, :, None] & (jnp.logical_not(diag)[None, None, :, None] | lower[None, :, None, :])


def attend(query_block, key_value_block, bids, vertical_row, srow):
    key_rows = key_value_block[..., :HEAD_SIZE].astype(jnp.float32)
    value_rows = key_value_block[..., HEAD_SIZE:].astype(jnp.float32)
    logit_matrix = jnp.einsum("unz,usyz->unsy", query_block.astype(jnp.float32), key_rows) * (1.0 / (HEAD_SIZE ** 0.5))
    mask = key_mask(bids, vertical_row, srow)
    logit_matrix = jnp.where(mask, logit_matrix, -1e30)
    top = jnp.max(logit_matrix, axis=(2, 3), keepdims=True)
    weights = jnp.where(mask, jnp.exp(logit_matrix - top), 0.0)
    total = jnp.sum(weights, axis=(2, 3))
    probabilities = lax.optimization_barrier(weights.astype(jnp.bfloat16))
    weighted_sum = jnp.einsum("wtef,wefs->wts", probabilities.astype(jnp.float32), value_rows)
    return (weighted_sum / total[..., None]).astype(jnp.bfloat16)


def reference(queries, kv_rows, vertical, slash):
    group = HEADS // KVH
    qall = queries.reshape(SEQ, HEADS, HEAD_SIZE)
    index_table = kv_rows.reshape(NB, BLK, KVH, 2 * HEAD_SIZE)

    def one_head(head):
        key_value_head = head // group
        vertical_row = vertical[head]
        srow = slash[head]
        qhead = lax.dynamic_index_in_dim(qall, head, 1, keepdims=False)
        qhead = qhead.reshape(N_SEQ, BLOCKS_PER_INDEX, BLK, HEAD_SIZE)

        def one_span(item):
            qspan, start = item
            bids = start + jnp.arange(BLOCKS_PER_INDEX, dtype=jnp.int32)
            vertical_index = jnp.broadcast_to(vertical_row[None, :], (BLOCKS_PER_INDEX, VERTICAL_COUNT))
            slash_index = jnp.clip(bids[:, None] - srow[None, :], 0, NB - 1)
            block_index = jnp.concatenate([vertical_index, slash_index], axis=1).astype(jnp.int32)
            key_value_block = index_table[block_index, :, key_value_head]
            return attend(qspan, key_value_block, bids, vertical_row, srow)

        starts = jnp.arange(N_SEQ, dtype=jnp.int32) * BLOCKS_PER_INDEX
        out = lax.map(one_span, (qhead, starts))
        return out.reshape(SEQ, HEAD_SIZE)

    result = lax.map(one_head, jnp.arange(HEADS, dtype=jnp.int32))
    return jnp.transpose(result, (1, 0, 2)).reshape(SEQ, HEADS * HEAD_SIZE)
```

```python
import functools
import math

import jax
import jax.numpy as jnp
from jax import lax
from jax.experimental import pallas as pl
from jax.experimental.pallas import tpu as pltpu
from jax.sharding import PartitionSpec as P

HEAD_SIZE = 128
BLK = 64
SMAX = 11
PIECE = 16
N_PIECES = (BLK // PIECE) * 2
LANES = 128
NEG = -1e30
SCALE = math.log2(math.e) / math.sqrt(HEAD_SIZE)
ANY = pl.BlockSpec(memory_space=pl.ANY)
VMEM_LIMIT = 48 * 1024 * 1024


def round_up(value, unit):
    return (value + unit - 1) // unit * unit


def last_two(a, b):
    return lax.dot_general(a, b, (((1,), (1,)), ((), ())), preferred_element_type=jnp.float32)


def head_rows(refs, source, block, group):
    rows = slice(block * BLK, (block + 1) * BLK)
    parts = []
    for h in range(group):
        lanes = slice(h * HEAD_SIZE, (h + 1) * HEAD_SIZE)
        part = refs[0][rows, lanes]
        if len(refs) == 2:
            part = jnp.where(source == 0, part, refs[1][rows, lanes])
        parts.append(part)
    return jnp.concatenate(parts, axis=0)


def selectors(n_query, group):
    shape = (n_query, group * BLK, LANES)
    head = lax.broadcasted_iota(jnp.int32, shape, 1) // BLK
    wanted = lax.broadcasted_iota(jnp.int32, shape, 0) * group + head
    return (lax.broadcasted_iota(jnp.int32, shape, 2) == wanted).astype(jnp.bfloat16)


def in_pipeline(count, scores_of, softmax_of, finish):
    scores = scores_of(0)
    waiting = None
    for n in range(count):
        following = scores_of(n + 1) if n + 1 < count else None
        current = softmax_of(n, scores)
        if waiting is not None:
            finish(*waiting)
        waiting = (n, *current)
        scores = following
    finish(*waiting)


def window_kernel(sizes, places, n_src, n_blk, group, pos_ref, *refs):
    n_pieces = len(sizes)
    pieces, refs = refs[:n_pieces], refs[n_pieces:]
    bias_ref, pick_ref, refs = refs[0], refs[1], refs[2:]
    q_refs, refs = refs[:n_src], refs[n_src:]
    acc_ref, ml_ref, table, kaug, vaug, sem = refs
    j, s = pl.program_id(0), pl.program_id(1)
    n_rows = table.shape[0]

    @pl.when((j == 0) & (s == 0))
    def _():
        copies = []
        for index in range(n_pieces):
            rows = pl.ds(places[index] * BLK, sizes[index])
            copies.append(
                pltpu.make_async_copy(pieces[index], table.at[rows], sem.at[index])
            )
        for copy in copies:
            copy.start()
        for copy in copies:
            copy.wait()

    @pl.when(s == 0)
    def _():
        col = pl.multiple_of(j * 2 * HEAD_SIZE, 2 * HEAD_SIZE)
        kaug[:, :HEAD_SIZE] = table[:, pl.ds(col, HEAD_SIZE)]
        vaug[:, :HEAD_SIZE] = table[:, pl.ds(col + HEAD_SIZE, HEAD_SIZE)]
        vaug[:, HEAD_SIZE:] = jnp.ones((n_rows, LANES), jnp.bfloat16)
        for w in range(n_rows // BLK):
            row = jnp.broadcast_to(bias_ref[0, w:w + 1, :], (BLK, LANES))
            kaug[w * BLK:(w + 1) * BLK, HEAD_SIZE:] = row.astype(jnp.bfloat16)

    core = pos_ref[0]
    base = 0 if n_src == 1 else jnp.where(s == 0, core, 1 - core) * n_blk
    span = (SMAX + 1) * BLK
    edge = span - LANES
    rows = group * BLK
    u = lax.broadcasted_iota(jnp.int32, (rows, LANES), 1) - (LANES - BLK)
    t = lax.broadcasted_iota(jnp.int32, (rows, LANES), 0) % BLK
    lane = lax.broadcasted_iota(jnp.int32, (rows, LANES), 1)

    def keys_of(n):
        return pl.ds(pl.multiple_of((base + n) * BLK, BLK), span)

    def scores_of(n):
        q = jnp.concatenate([head_rows(q_refs, s, n, group), pick_ref[base + n]], axis=1)
        return last_two(q, kaug[keys_of(n), :])

    def softmax_of(n, scores):
        last = jnp.where(u > t, NEG, scores[:, edge:])
        scores = jnp.concatenate([scores[:, :edge], last], axis=1)
        top = jnp.max(scores, axis=1, keepdims=True)
        return top, jnp.exp2((scores - top) * SCALE).astype(jnp.bfloat16)

    def finish(n, top, weights):
        total = jnp.dot(weights, vaug[keys_of(n), :], preferred_element_type=jnp.float32)
        acc_ref[0, 0, n] = total[:, :HEAD_SIZE]
        ml_ref[0, 0, n] = jnp.where(lane < LANES // 2, top, total[:, HEAD_SIZE:])

    in_pipeline(n_blk, scores_of, softmax_of, finish)


def window_part(pos, pieces, places, bias, picks, queries, q_recv, n_kv, n_src, n_blk, group, n_win):
    width = group * HEAD_SIZE
    rows = group * BLK
    n_rows = n_win * BLK
    q_specs = [pl.BlockSpec((n_blk * BLK, width), lambda j, s, pos: (0, pos[0] * n_kv + j))]
    q_args = [queries]
    if n_src == 2:
        q_specs.append(pl.BlockSpec((n_blk * BLK, width), lambda j, s, pos: (0, j)))
        q_args.append(q_recv)
    out_spec = pl.BlockSpec((1, 1, n_blk, rows, LANES), lambda j, s, pos: (j, s, 0, 0, 0))
    out_shape = jax.ShapeDtypeStruct((n_kv, n_src, n_blk, rows, LANES), jnp.float32)
    sizes = [piece.shape[0] for piece in pieces]
    keys = n_kv * n_src * n_blk * rows * (SMAX + 1) * BLK
    return pl.pallas_call(
        functools.partial(window_kernel, sizes, places, n_src, n_blk, group),
        grid_spec=pltpu.PrefetchScalarGridSpec(
            num_scalar_prefetch=1,
            grid=(n_kv, n_src),
            in_specs=[ANY] * len(pieces)
            + [
                pl.BlockSpec((1, bias.shape[1], LANES), lambda j, s, pos: (j, 0, 0)),
                pl.BlockSpec(memory_space=pltpu.VMEM),
            ]
            + q_specs,
            out_specs=[out_spec, out_spec],
            scratch_shapes=[
                pltpu.VMEM((n_rows, n_kv * 2 * HEAD_SIZE), jnp.bfloat16),
                pltpu.VMEM((n_rows, 2 * LANES), jnp.bfloat16),
                pltpu.VMEM((n_rows, 2 * LANES), jnp.bfloat16),
                pltpu.SemaphoreType.DMA((len(pieces),)),
            ],
        ),
        out_shape=[out_shape, out_shape],
        compiler_params=pltpu.CompilerParams(vmem_limit_bytes=VMEM_LIMIT),
        cost_estimate=pl.CostEstimate(
            flops=keys * 1024, bytes_accessed=16 * 1024 * 1024, transcendentals=keys
        ),
    )(pos, *pieces, bias, picks, *q_args)


def vertical_kernel(sources, first_kv, n_vert, group, n_blk, n_src, n_dst, other, pos_ref, *refs):
    n_pieces = max(source[0] for source in sources) + 1
    pieces, refs = refs[:n_pieces], refs[n_pieces:]
    bias_ref, pick_ref, refs = refs[0], refs[1], refs[2:]
    q_refs, refs = refs[:n_src], refs[n_src:]
    acc_ref, ml_ref, refs = refs[0], refs[1], refs[2:]
    outs, (table, kaug, vaug, sem) = refs[:n_src], refs[n_src:]
    j, s = pl.program_id(0), pl.program_id(1)
    per_dst = n_blk // n_dst
    n_keys = kaug.shape[0]
    group_rows = n_vert * PIECE

    @pl.when(s == 0)
    def _():
        copies = []
        for index, (piece, part) in enumerate(sources):
            copies.append(
                pltpu.make_async_copy(
                    pieces[piece].at[part, first_kv + j], table.at[pos_ref[2 + index]], sem.at[index]
                )
            )
        for copy in copies:
            copy.start()
        used = (N_PIECES // 2) * group_rows
        if used < n_keys:
            empty = (n_keys - used, LANES)
            kaug[used:, :HEAD_SIZE] = jnp.zeros(empty, jnp.bfloat16)
            vaug[used:, :HEAD_SIZE] = jnp.zeros(empty, jnp.bfloat16)
            kaug[used:, HEAD_SIZE:] = jnp.full(empty, NEG, jnp.bfloat16)
        vaug[:, HEAD_SIZE:] = jnp.ones((n_keys, LANES), jnp.bfloat16)
        for unit in range(n_vert):
            row = jnp.broadcast_to(bias_ref[0, unit:unit + 1, :], (PIECE, LANES))
            row = row.astype(jnp.bfloat16)
            for rg in range(N_PIECES // 2):
                at = rg * group_rows + unit * PIECE
                kaug[at:at + PIECE, HEAD_SIZE:] = row
        for copy in copies:
            copy.wait()
        for rg in range(N_PIECES // 2):
            at = slice(rg * group_rows, (rg + 1) * group_rows)
            kaug[at, :HEAD_SIZE] = table[2 * rg]
            vaug[at, :HEAD_SIZE] = table[2 * rg + 1]

    core, tp_pos = pos_ref[0], pos_ref[1]
    base = 0
    if n_dst > 1:
        base = (1 - tp_pos if other else tp_pos) * per_dst
    if n_src > 1:
        base = base + jnp.where(s == 0, core, 1 - core) * n_blk

    def scores_of(n):
        q = jnp.concatenate([head_rows(q_refs, s, n, group), pick_ref[base + n]], axis=1)
        return last_two(q, kaug[...])

    def softmax_of(n, scores):
        old_top = ml_ref[0, 0, n][:, :1]
        top = jnp.maximum(old_top, jnp.max(scores, axis=1, keepdims=True))
        shrink = jnp.exp2((old_top - top) * SCALE)
        return shrink, jnp.exp2((scores - top) * SCALE).astype(jnp.bfloat16)

    def finish(n, shrink, weights):
        total = jnp.dot(weights, vaug[...], preferred_element_type=jnp.float32)
        old_total = ml_ref[0, 0, n][:, LANES // 2:LANES // 2 + 1]
        weighted = total[:, :HEAD_SIZE] + acc_ref[0, 0, n] * shrink
        out = (weighted / (total[:, HEAD_SIZE:] + old_total * shrink)).astype(jnp.bfloat16)
        out = jnp.concatenate([out[h * BLK:(h + 1) * BLK] for h in range(group)], axis=1)
        for source in range(n_src):

            @pl.when(s == source)
            def _():
                outs[source][n * BLK:(n + 1) * BLK, :] = out

    in_pipeline(per_dst, scores_of, softmax_of, finish)


def vertical_part(
    pos, pieces, sources, first_kv, kvs, bias, picks, queries, q_recv, state,
    n_kv, n_src, n_dst, other, n_blk, group, n_vert,
):
    width = group * HEAD_SIZE
    rows = group * BLK
    per_dst = n_blk // n_dst
    n_keys = round_up(n_vert * BLK, LANES)

    def place(pos):
        if n_dst == 1:
            return 0
        return 1 - pos[1] if other else pos[1]

    q_specs = [
        pl.BlockSpec(
            (per_dst * BLK, width), lambda j, s, pos: (place(pos), pos[0] * n_kv + first_kv + j)
        )
    ]
    q_args = [queries]
    if n_src == 2:
        q_specs.append(
            pl.BlockSpec((per_dst * BLK, width), lambda j, s, pos: (place(pos), first_kv + j))
        )
        q_args.append(q_recv)
    state_spec = pl.BlockSpec(
        (1, 1, per_dst, rows, LANES), lambda j, s, pos: (first_kv + j, s, place(pos), 0, 0)
    )
    out_spec = pl.BlockSpec((per_dst * BLK, width), lambda j, s, pos: (0, j))
    out_shape = jax.ShapeDtypeStruct((per_dst * BLK, width * kvs), jnp.bfloat16)
    keys = kvs * n_src * per_dst * rows * n_keys
    return pl.pallas_call(
        functools.partial(
            vertical_kernel, sources, first_kv, n_vert, group, n_blk, n_src, n_dst, other
        ),
        grid_spec=pltpu.PrefetchScalarGridSpec(
            num_scalar_prefetch=1,
            grid=(kvs, n_src),
            in_specs=[ANY] * len(pieces)
            + [
                pl.BlockSpec((1, bias.shape[1], LANES), lambda j, s, pos: (first_kv + j, 0, 0)),
                pl.BlockSpec(memory_space=pltpu.VMEM),
            ]
            + q_specs
            + [state_spec, state_spec],
            out_specs=[out_spec] * n_src,
            scratch_shapes=[
                pltpu.VMEM((N_PIECES, n_vert * PIECE, LANES), jnp.bfloat16),
                pltpu.VMEM((n_keys, 2 * LANES), jnp.bfloat16),
                pltpu.VMEM((n_keys, 2 * LANES), jnp.bfloat16),
                pltpu.SemaphoreType.DMA((N_PIECES,)),
            ],
        ),
        out_shape=[out_shape] * n_src,
        compiler_params=pltpu.CompilerParams(vmem_limit_bytes=VMEM_LIMIT),
        cost_estimate=pl.CostEstimate(
            flops=keys * 1024, bytes_accessed=8 * 1024 * 1024, transcendentals=keys
        ),
    )(pos, *pieces, bias, picks, *q_args, *state)


def select_kernel(n_kv, n_vert, index_ref, table, *outs):
    for j in range(n_kv):
        for unit in range(n_vert):
            outs[j][unit * PIECE:(unit + 1) * PIECE, :] = table[index_ref[j * n_vert + unit]]


def select_units(index, table, n_kv, n_vert):
    return pl.pallas_call(
        functools.partial(select_kernel, n_kv, n_vert),
        in_specs=[
            pl.BlockSpec(memory_space=pltpu.SMEM),
            pl.BlockSpec(memory_space=pltpu.VMEM),
        ],
        out_specs=[pl.BlockSpec(memory_space=pltpu.VMEM)] * n_kv,
        out_shape=[jax.ShapeDtypeStruct((n_vert * PIECE, LANES), jnp.bfloat16)] * n_kv,
        compiler_params=pltpu.CompilerParams(vmem_limit_bytes=8 * 1024 * 1024),
    )(index, table)


def assemble_kernel(width, n, column_ref, *refs):
    for index in range(n):
        start = pl.multiple_of(column_ref[index] * width, width)
        refs[n][:, pl.ds(start, width)] = refs[index][...]


def assemble(columns, pieces):
    n = len(pieces)
    rows, width = pieces[0].shape
    step = 32
    return pl.pallas_call(
        functools.partial(assemble_kernel, width, n),
        grid_spec=pltpu.PrefetchScalarGridSpec(
            num_scalar_prefetch=1,
            grid=(rows // step,),
            in_specs=[pl.BlockSpec((step, width), lambda i, columns: (i, 0))] * n,
            out_specs=pl.BlockSpec((step, width * n), lambda i, columns: (i, 0)),
        ),
        out_shape=jax.ShapeDtypeStruct((rows, width * n), pieces[0].dtype),
    )(columns, *pieces)


def mask_tables(vert, slash, first, n_query, n_win, n_vert, n_blocks):
    n_kv, group = vert.shape[:2]
    blocks = jnp.arange(n_blocks, dtype=jnp.int32)
    present = jnp.any(vert.reshape(n_kv, -1)[:, :, None] == blocks, axis=1)
    before = blocks[None, :] < blocks[:, None]
    rank = jnp.sum((present[:, None, :] & before[None]).astype(jnp.int32), axis=2)
    unit = jnp.arange(n_vert, dtype=jnp.int32)
    here = present[:, None, :] & (rank[:, None, :] == unit[None, :, None])
    units = jnp.sum(jnp.where(here, blocks, 0), axis=2)

    query = first + jnp.arange(n_query, dtype=jnp.int32)
    window = first - SMAX + jnp.arange(n_win, dtype=jnp.int32)
    offset = query[None, :] - window[:, None]
    by_slash = jnp.any(offset[None, :, :, None, None] == slash[:, None, None, :, :], axis=4)
    by_vert = jnp.any(window[None, :, None, None] == vert[:, None, :, :], axis=3)
    near = (offset >= 0) & (offset <= SMAX) & (window >= 0)[:, None]
    live_w = near[None, :, :, None] & (by_slash | by_vert[:, :, None, :])
    listed = jnp.any(units[:, :, None, None] == vert[:, None, :, :], axis=3)
    far = query[None, None, :] - units[:, :, None] > SMAX
    live_v = far[:, :, :, None] & listed[:, :, None, :]

    def as_rows(live):
        rows = live.shape[1]
        bias = jnp.where(live, 0.0, NEG).astype(jnp.float32).reshape(n_kv, rows, n_query * group)
        pad = ((0, 0), (0, round_up(rows, 8) - rows), (0, LANES - n_query * group))
        return jnp.pad(bias, pad)

    return units, as_rows(live_w), as_rows(live_v)


def paired(queries, kv_rows, vertical, slash):
    n_seq = lax.axis_size("seq")
    n_chip = n_seq // 2
    n_far = n_chip // 2
    tok = queries.shape[0]
    n_blk = tok // BLK
    seq_pos, tp_pos = lax.axis_index("seq"), lax.axis_index("tp")
    core, chip = seq_pos % 2, seq_pos // 2
    near, far = chip % 2, chip // 2
    heads_loc = vertical.shape[0] // 2
    kv_loc = kv_rows.shape[1] // (2 * HEAD_SIZE)
    group = heads_loc // kv_loc
    n_kv = kv_loc // 2
    heads = n_kv * group
    n_blocks = n_seq * n_blk
    n_vert = vertical.shape[1] * 3 // 2 - 1
    n_query = 2 * n_blk
    n_win = n_query + SMAX
    kv_width = n_kv * 2 * HEAD_SIZE
    q_width = heads * HEAD_SIZE

    def by_chip(array, target):
        pairs = []
        for source in range(n_seq):
            to = target(source // 2)
            if to is not None:
                pairs.append((source, 2 * to + source % 2))
        return lax.ppermute(array, "seq", pairs)

    split = kv_rows.reshape(n_blk, BLK // PIECE, PIECE, 2, n_kv, 2, LANES)
    split = jnp.transpose(split, (1, 5, 3, 0, 4, 2, 6)).reshape(n_seq, n_blk * n_kv, PIECE, LANES)
    held = lax.all_to_all(split, "seq", split_axis=0, concat_axis=0, tiled=True)
    held = held.reshape(n_blocks * n_kv, PIECE, LANES)

    to_pair = jnp.concatenate(
        [
            lax.dynamic_slice_in_dim(queries, (1 - core) * q_width, q_width, 1),
            lax.dynamic_slice_in_dim(kv_rows, (1 - core) * kv_width, kv_width, 1),
        ],
        axis=1,
    )
    from_pair = lax.ppermute(to_pair, "seq", [(i, i ^ 1) for i in range(n_seq)])
    mine = lax.dynamic_slice_in_dim(kv_rows, core * kv_width, kv_width, 1)
    theirs = from_pair[:, q_width:]
    here = jnp.where(
        core == 0,
        jnp.concatenate([mine, theirs], axis=0),
        jnp.concatenate([theirs, mine], axis=0),
    )
    extra = SMAX - n_query
    before = by_chip(here, lambda c: c + 1 if c + 1 < n_chip else None)
    back = by_chip(here[-extra * BLK:], lambda c: c + 2 if c + 2 < n_chip else None)

    first_head = tp_pos * heads_loc + core * heads
    my_vert = lax.dynamic_slice_in_dim(vertical, first_head, heads, 0).reshape(n_kv, group, -1)
    my_slash = lax.dynamic_slice_in_dim(slash, first_head, heads, 0).reshape(n_kv, group, -1)
    units, bias_w, bias_v = mask_tables(
        my_vert, my_slash, chip * n_query, n_query, n_win, n_vert, n_blocks
    )
    picks = selectors(n_query, group)

    index = (units * n_kv + jnp.arange(n_kv, dtype=jnp.int32)[:, None]).reshape(-1)
    picked = jnp.stack(select_units(index, held, n_kv, n_vert))
    beside = by_chip(picked, lambda c: c ^ 1)
    both = jnp.where(near == 0, jnp.stack([picked, beside]), jnp.stack([beside, picked]))
    pieces, sources, slots = [both], [(0, 0), (0, 1)], [2 * far, 2 * far + 1]
    for step in range(1, n_far):
        pieces.append(by_chip(both, lambda c: (c + 2 * step) % n_chip))
        sources += [(step, 0), (step, 1)]
        owner = (far - step) % n_far
        slots += [2 * owner, 2 * owner + 1]

    pos = jnp.stack([core, tp_pos] + slots).astype(jnp.int32)
    state = window_part(
        pos, [here, before, back], [SMAX, extra, 0], bias_w, picks, queries, from_pair,
        n_kv, 2, n_blk, group, n_win,
    )

    def swap(array, other_core, other_tp):
        pairs = []
        for source in range(n_seq):
            for t in range(2):
                pairs.append((source * 2 + t, (source ^ other_core) * 2 + (t ^ other_tp)))
        return lax.ppermute(array, ("seq", "tp"), pairs)

    results, columns = [], []
    for other_tp in (1, 0):
        outs = vertical_part(
            pos, pieces, sources, 0, n_kv, bias_v, picks, queries, from_pair, state,
            n_kv, 2, 2, other_tp, n_blk, group, n_vert,
        )
        for other_core in range(2):
            piece = outs[other_core]
            if other_core or other_tp:
                piece = swap(piece, other_core, other_tp)
            results.append(piece)
            from_tp = 1 - tp_pos if other_tp else tp_pos
            from_core = 1 - core if other_core else core
            columns.append(from_tp * 2 + from_core)
    return assemble(jnp.stack(columns).astype(jnp.int32), results)


def gathered(queries, kv_rows, vertical, slash):
    n_seq, n_tp = lax.axis_size("seq"), lax.axis_size("tp")
    tok = queries.shape[0]
    n_blk = tok // BLK
    seq_pos, tp_pos = lax.axis_index("seq"), lax.axis_index("tp")
    heads = vertical.shape[0] // n_tp
    n_kv = kv_rows.shape[1] // (2 * HEAD_SIZE)
    group = heads // n_kv
    n_blocks = n_seq * n_blk
    n_vert = vertical.shape[1] * 3 // 2 - 1
    n_win = n_blk + SMAX
    first = seq_pos * n_blk
    my_vert = lax.dynamic_slice_in_dim(vertical, tp_pos * heads, heads, 0)
    my_slash = lax.dynamic_slice_in_dim(slash, tp_pos * heads, heads, 0)
    units, bias_w, bias_v = mask_tables(
        my_vert.reshape(n_kv, group, -1), my_slash.reshape(n_kv, group, -1),
        first, n_blk, n_win, n_vert, n_blocks,
    )
    picks = selectors(n_blk, group)
    full = lax.all_gather(kv_rows, "seq", axis=0, tiled=True)
    padded = jnp.pad(full, ((SMAX * BLK, 0), (0, 0)))
    window = lax.dynamic_slice_in_dim(padded, first * BLK, n_win * BLK, 0)
    pos = jnp.stack([jnp.int32(0), tp_pos] + [jnp.int32(i) for i in range(N_PIECES)])
    state = window_part(
        pos, [window], [0], bias_w, picks, queries, None, n_kv, 1, n_blk, group, n_win
    )
    blocks = full.reshape(n_blocks, BLK // PIECE, PIECE, n_kv, 2, LANES)
    listed = jnp.stack([blocks[units[j], :, :, j] for j in range(n_kv)])
    listed = jnp.transpose(listed, (2, 4, 0, 1, 3, 5))
    listed = listed.reshape(N_PIECES, n_kv, n_vert * PIECE, LANES)
    (attended,) = vertical_part(
        pos, [listed], [(0, i) for i in range(N_PIECES)], 0, n_kv, bias_v, picks, queries, None,
        state, n_kv, 1, 1, 0, n_blk, group, n_vert,
    )
    return lax.all_to_all(attended, "tp", split_axis=0, concat_axis=1, tiled=True)


def per_device(queries, kv_rows, vertical, slash):
    n_seq, n_tp = lax.axis_size("seq"), lax.axis_size("tp")
    kv_loc = kv_rows.shape[1] // (2 * HEAD_SIZE)
    n_blk = queries.shape[0] // BLK
    if n_seq == 2 * N_PIECES and n_tp == 2 and kv_loc % 2 == 0 and n_blk == 4:
        return paired(queries, kv_rows, vertical, slash)
    return gathered(queries, kv_rows, vertical, slash)


def solution(mesh):
    return jax.shard_map(
        per_device,
        mesh=mesh,
        in_specs=(P("seq", "tp"), P("seq", "tp"), P(), P()),
        out_specs=P(("seq", "tp"), None),
        check_vma=False,
    )
```

```python
import functools
import math

import jax
import jax.numpy as jnp
from jax import lax
from jax.experimental import pallas as pl
from jax.experimental.pallas import tpu as pltpu
from jax.sharding import PartitionSpec as P

HEAD_SIZE = 128
BLK = 64
SMAX = 11
PIECE = 16
N_PIECES = (BLK // PIECE) * 2
LANES = 128
NEG = -1e30
SCALE = math.log2(math.e) / math.sqrt(HEAD_SIZE)
LOG_SCALE = math.sqrt(HEAD_SIZE)
ANY = pl.BlockSpec(memory_space=pl.ANY)


VMEM_LIMIT = 32 * 1024 * 1024
ALL_VMEM = 60 * 1024 * 1024


def round_up(value, unit):
    return (value + unit - 1) // unit * unit


def head_rows(ref, block, group):
    rows = slice(block * BLK, (block + 1) * BLK)
    heads = [ref[rows, h * HEAD_SIZE:(h + 1) * HEAD_SIZE] for h in range(group)]
    return jnp.concatenate(heads, axis=0)


def with_selector(q, block, group):
    shape = (q.shape[0], LANES)
    wanted = lax.broadcasted_iota(jnp.int32, shape, 0) // BLK + block * group
    pick = lax.broadcasted_iota(jnp.int32, shape, 1) == wanted
    return jnp.concatenate([q, jnp.where(pick, 1.0, 0.0).astype(jnp.bfloat16)], axis=1)


def in_pipeline(count, scores_of, softmax_of, finish):
    scores = scores_of(0)
    waiting = None
    for n in range(count):
        following = scores_of(n + 1) if n + 1 < count else None
        current = softmax_of(n, scores)
        if waiting is not None:
            finish(*waiting)
        waiting = (n, *current)
        scores = following
    finish(*waiting)


def tiles(array):
    return [array[:, at:at + LANES] for at in range(0, array.shape[1], LANES)]


def row_top(parts):
    top = functools.reduce(jnp.maximum, parts)
    return jnp.broadcast_to(jnp.max(top, axis=1, keepdims=True), top.shape)


def exponents(parts, top):
    return jnp.concatenate(
        [jnp.exp2((part - top) * SCALE).astype(jnp.bfloat16) for part in parts], axis=1
    )


def start_all(copies):
    for copy in copies:
        copy.start()


def wait_all(copies):
    for copy in copies:
        copy.wait()


def spread_mask(table, block_of_key, n_keys):
    shape = (LANES, n_keys)
    key = lax.broadcasted_iota(jnp.int32, shape, 1)
    own = lax.broadcasted_iota(jnp.int32, shape, 0) == block_of_key(key)
    own = jnp.where(own, 1.0, 0.0).astype(jnp.bfloat16)
    return jnp.dot(table, own, preferred_element_type=jnp.float32).astype(jnp.bfloat16)


def window_kernel(sizes, places, n_kv, n_src, n_blk, group, pos_ref, *refs):
    n_pieces = len(sizes)
    pieces, refs = refs[:n_pieces], refs[n_pieces:]
    bias_ref, refs = refs[0], refs[1:]
    q_in, refs = refs[:n_src], refs[n_src:]
    acc_out, lse_out, table, mask, kaug, vaug, q_ref, acc_ref, lse_ref, sem, turn_sem = refs
    core = pos_ref[0]
    n_rows = table.shape[1]
    n_lanes = kaug.shape[3]
    n_mask = bias_ref.shape[1]
    width = group * HEAD_SIZE
    span = (SMAX + 1) * BLK
    rows = group * BLK
    tok = n_blk * BLK
    n_pairs = n_src * n_blk // 2
    count = iter(range(sem.shape[0]))

    loads = []
    for j in range(n_kv):
        mine = []
        lanes = pl.ds(j * 2 * HEAD_SIZE, 2 * HEAD_SIZE)
        for index in range(n_pieces):
            at = pl.ds(places[index] * BLK, sizes[index])
            mine.append((pieces[index].at[:, lanes], table.at[j, at]))
        mine.append((bias_ref.at[j], mask.at[j]))
        first = pl.multiple_of((core * n_kv + j) * width, width)
        q_lanes = [pl.ds(first, width), pl.ds(j * width, width)]
        for source in range(n_src):
            at = pl.ds((j * n_src + source) * tok, tok)
            mine.append((q_in[source].at[:, q_lanes[source]], q_ref.at[at]))
        loads.append([pltpu.make_async_copy(*pair, sem.at[next(count)]) for pair in mine])
    for mine in loads:
        start_all(mine)
    for j in range(n_kv):
        vaug[j, :, HEAD_SIZE:] = jnp.ones((n_rows, LANES), jnp.bfloat16)
        for odd in range(2):
            kaug[j, odd, HEAD_SIZE + n_mask:, :] = jnp.zeros((LANES - n_mask, n_lanes), jnp.bfloat16)
    for j in range(n_kv):
        wait_all(loads[j])
        for odd in range(2):
            kaug[j, odd, :HEAD_SIZE, :] = table[j, odd * BLK:odd * BLK + n_lanes, :HEAD_SIZE].T
            kaug[j, odd, HEAD_SIZE:HEAD_SIZE + n_mask, :] = spread_mask(
                mask[j], lambda key: key // BLK + odd, n_lanes
            )
        vaug[j, :, :HEAD_SIZE] = table[j, :, HEAD_SIZE:]

    u = lax.broadcasted_iota(jnp.int32, (rows, LANES), 1) - (LANES - BLK)
    t = lax.broadcasted_iota(jnp.int32, (rows, LANES), 0) % BLK

    def stores(turn):
        blocks = pl.ds(2 * turn, 2)
        return [
            pltpu.make_async_copy(acc_ref.at[blocks], acc_out.at[blocks], turn_sem.at[turn, 0]),
            pltpu.make_async_copy(lse_ref.at[blocks], lse_out.at[blocks], turn_sem.at[turn, 1]),
        ]

    def two_blocks(turn, carry):
        j, pair = turn // n_pairs, turn % n_pairs
        base = 2 * pair
        if n_src == 2:
            per = n_blk // 2
            base = jnp.where(pair < per, core, 1 - core) * n_blk + 2 * (pair % per)
        q_rows = q_ref.at[pl.ds(pl.multiple_of(2 * turn * BLK, 2 * BLK), 2 * BLK)]
        even = pl.ds(pl.multiple_of(base * BLK, LANES), span)

        def scores_of(n):
            q = with_selector(head_rows(q_rows, n, group), base + n, group)
            return jnp.dot(q, kaug[j, n, :, even], preferred_element_type=jnp.float32)

        def softmax_of(n, scores):
            parts = tiles(scores)
            parts[-1] = jnp.where(u > t, NEG, parts[-1])
            top = row_top(parts)
            return top, exponents(parts, top)

        def finish(n, top, weights):
            at = pl.ds(pl.multiple_of((base + n) * BLK, BLK), span)
            total = jnp.dot(weights, vaug[j, at, :], preferred_element_type=jnp.float32)
            acc_ref[2 * turn + n] = total[:, :HEAD_SIZE] / total[:, HEAD_SIZE:]
            lse_ref[2 * turn + n] = top + jnp.log(total[:, HEAD_SIZE:]) * LOG_SCALE

        in_pipeline(2, scores_of, softmax_of, finish)
        start_all(stores(turn))
        return carry

    lax.fori_loop(0, n_kv * n_pairs, two_blocks, 0)
    for turn in range(n_kv * n_pairs):
        wait_all(stores(turn))


def window_part(pos, pieces, places, bias, queries, q_recv, n_kv, n_src, n_blk, group, n_win):
    width = group * HEAD_SIZE
    rows = group * BLK
    n_rows = n_win * BLK
    n_turns = n_kv * n_src * n_blk // 2
    q_args = [queries] if n_src == 1 else [queries, q_recv]
    out_shape = jax.ShapeDtypeStruct((2 * n_turns, rows, LANES), jnp.float32)
    sizes = [piece.shape[0] for piece in pieces]
    keys = 2 * n_turns * rows * (SMAX + 1) * BLK
    return pl.pallas_call(
        functools.partial(window_kernel, sizes, places, n_kv, n_src, n_blk, group),
        in_specs=[pl.BlockSpec(memory_space=pltpu.SMEM)]
        + [ANY] * (len(pieces) + 1 + n_src),
        out_specs=[ANY, ANY],
        scratch_shapes=[
            pltpu.VMEM((n_kv, n_rows, 2 * HEAD_SIZE), jnp.bfloat16),
            pltpu.VMEM(bias.shape, jnp.bfloat16),
            pltpu.VMEM((n_kv, 2, 2 * LANES, n_rows - BLK), jnp.bfloat16),
            pltpu.VMEM((n_kv, n_rows, 2 * LANES), jnp.bfloat16),
            pltpu.VMEM((2 * n_turns * BLK, width), jnp.bfloat16),
            pltpu.VMEM(out_shape.shape, jnp.float32),
            pltpu.VMEM(out_shape.shape, jnp.float32),
            pltpu.SemaphoreType.DMA((n_kv * (len(pieces) + 1 + n_src),)),
            pltpu.SemaphoreType.DMA((n_turns, 2)),
        ],
        out_shape=[out_shape, out_shape],
        compiler_params=pltpu.CompilerParams(vmem_limit_bytes=VMEM_LIMIT),
        cost_estimate=pl.CostEstimate(
            flops=keys * 1024, bytes_accessed=16 * 1024 * 1024, transcendentals=keys
        ),
    )(pos, *pieces, bias, *q_args)


def vertical_kernel(sources, kvs, n_kv, n_vert, group, n_blk, n_src, n_dst, other, pos_ref, *refs):
    n_pieces = max(source[0] for source in sources) + 1
    n_mine = len(kvs)
    pieces, refs = refs[:n_pieces], refs[n_pieces:]
    bias_ref, refs = refs[0], refs[1:]
    q_in, refs = refs[:n_src], refs[n_src:]
    acc_in, lse_in, refs = refs[0], refs[1], refs[2:]
    outs_ref, refs = refs[:n_mine * n_src], refs[n_mine * n_src:]
    table, mask, kaug, vaug, q_ref, acc_ref, lse_ref, out_ref, sem, turn_sem = refs
    core, tp_pos = pos_ref[0], pos_ref[1]
    per_dst = n_blk // n_dst
    n_keys = vaug.shape[1]
    n_mask = bias_ref.shape[1]
    group_rows = n_vert * PIECE
    used = (N_PIECES // 2) * group_rows
    width = group * HEAD_SIZE
    base = 0
    if n_dst > 1:
        base = (1 - tp_pos if other else tp_pos) * per_dst
    count = iter(range(sem.shape[0]))

    loads = []
    for m, j in enumerate(kvs):
        for index, (piece, part) in enumerate(sources):
            slot = pos_ref[2 + index]
            rows = pl.ds(pl.multiple_of((slot // 2) * group_rows, PIECE), group_rows)
            loads.append(
                pltpu.make_async_copy(
                    pieces[piece].at[part, j], table.at[m, slot % 2, rows], sem.at[next(count)]
                )
            )
        loads.append(pltpu.make_async_copy(bias_ref.at[j], mask.at[m], sem.at[next(count)]))
    q_rows = pl.ds(pl.multiple_of(base * BLK, BLK), per_dst * BLK)

    def turn_loads(m, source, turn):
        j = kvs[m]
        first = pl.multiple_of((core * n_kv + j) * width, width)
        q_lanes = [pl.ds(first, width), pl.ds(j * width, width)]
        blocks = pl.ds((j * n_src + source) * n_blk + base, per_dst)
        return [
            pltpu.make_async_copy(
                q_in[source].at[q_rows, q_lanes[source]], q_ref.at[turn], turn_sem.at[turn, 0]
            ),
            pltpu.make_async_copy(
                acc_in.at[blocks], acc_ref.at[turn], turn_sem.at[turn, 1]
            ),
            pltpu.make_async_copy(
                lse_in.at[blocks], lse_ref.at[turn], turn_sem.at[turn, 2]
            ),
        ]

    start_all(loads)
    for m in range(n_mine):
        for source in range(n_src):
            start_all(turn_loads(m, source, m * n_src + source))
    for m in range(n_mine):
        if used < n_keys:
            empty = jnp.zeros((n_keys - used, LANES), jnp.bfloat16)
            table[m, 0, used:] = empty
            table[m, 1, used:] = empty
        vaug[m, :, HEAD_SIZE:] = jnp.ones((n_keys, LANES), jnp.bfloat16)
        kaug[m, HEAD_SIZE + n_mask:, :] = jnp.zeros((LANES - n_mask, n_keys), jnp.bfloat16)
    wait_all(loads)
    for m in range(n_mine):
        kaug[m, :HEAD_SIZE, :] = table[m, 0].T
        kaug[m, HEAD_SIZE:HEAD_SIZE + n_mask, :] = spread_mask(
            mask[m], lambda key: key % group_rows // PIECE, n_keys
        )
        if used < n_keys:
            kaug[m, HEAD_SIZE:HEAD_SIZE + n_mask, used:] = jnp.full((n_mask, n_keys - used), NEG, jnp.bfloat16)
        vaug[m, :, :HEAD_SIZE] = table[m, 1]

    def one_turn(turn, carry):
        j = turn // n_src
        first_block = base
        if n_src == 2:
            first_block = base + jnp.where(turn % 2 == 0, core, 1 - core) * n_blk
        wait_all(turn_loads(0, 0, turn))

        def scores_of(n):
            q = with_selector(head_rows(q_ref.at[turn], n, group), first_block + n, group)
            return jnp.dot(q, kaug[j], preferred_element_type=jnp.float32)

        def softmax_of(n, scores):
            old = lse_ref[turn, n]
            parts = tiles(scores)
            top = jnp.maximum(old, row_top(parts))
            return jnp.exp2((old - top) * SCALE), exponents(parts, top)

        def finish(n, shrink, weights):
            total = jnp.dot(weights, vaug[j], preferred_element_type=jnp.float32)
            weighted = total[:, :HEAD_SIZE] + acc_ref[turn, n] * shrink
            out = (weighted / (total[:, HEAD_SIZE:] + shrink)).astype(jnp.bfloat16)
            for h in range(group):
                lanes = slice(h * HEAD_SIZE, (h + 1) * HEAD_SIZE)
                out_ref[turn, n * BLK:(n + 1) * BLK, lanes] = out[h * BLK:(h + 1) * BLK]

        in_pipeline(per_dst, scores_of, softmax_of, finish)
        return carry

    lax.fori_loop(0, n_mine * n_src, one_turn, 0)
    stores = [
        pltpu.make_async_copy(out_ref.at[turn], outs_ref[turn], turn_sem.at[turn, 3])
        for turn in range(n_mine * n_src)
    ]
    start_all(stores)
    wait_all(stores)


def vertical_part(
    pos, pieces, sources, kvs, bias, queries, q_recv, state, n_kv, n_src, n_dst, other, n_blk, group, n_vert
):
    n_mine = len(kvs)
    n_turns = n_mine * n_src
    width = group * HEAD_SIZE
    rows = group * BLK
    per_dst = n_blk // n_dst
    n_keys = round_up(n_vert * BLK, LANES)
    q_args = [queries] if n_src == 1 else [queries, q_recv]
    out_shape = jax.ShapeDtypeStruct((per_dst * BLK, width), jnp.bfloat16)
    keys = n_turns * per_dst * rows * n_keys
    args = [*pieces, bias, *q_args, *state]
    return pl.pallas_call(
        functools.partial(
            vertical_kernel, sources, kvs, n_kv, n_vert, group, n_blk, n_src, n_dst, other
        ),
        in_specs=[pl.BlockSpec(memory_space=pltpu.SMEM)] + [ANY] * len(args),
        out_specs=[ANY] * n_turns,
        scratch_shapes=[
            pltpu.VMEM((n_mine, 2, n_keys, LANES), jnp.bfloat16),
            pltpu.VMEM((n_mine,) + bias.shape[1:], jnp.bfloat16),
            pltpu.VMEM((n_mine, 2 * LANES, n_keys), jnp.bfloat16),
            pltpu.VMEM((n_mine, n_keys, 2 * LANES), jnp.bfloat16),
            pltpu.VMEM((n_turns, per_dst * BLK, width), jnp.bfloat16),
            pltpu.VMEM((n_turns, per_dst, rows, LANES), jnp.float32),
            pltpu.VMEM((n_turns, per_dst, rows, LANES), jnp.float32),
            pltpu.VMEM((n_turns, per_dst * BLK, width), jnp.bfloat16),
            pltpu.SemaphoreType.DMA((n_mine * (N_PIECES + 1),)),
            pltpu.SemaphoreType.DMA((n_turns, 4)),
        ],
        out_shape=[out_shape] * n_turns,
        compiler_params=pltpu.CompilerParams(vmem_limit_bytes=(16 + round_up(8 * n_keys // 768, 8)) * 1024 * 1024),
        cost_estimate=pl.CostEstimate(
            flops=keys * 1024, bytes_accessed=8 * 1024 * 1024, transcendentals=keys
        ),
    )(pos, *args)


def split_kernel(n_kv, kv_ref, out_ref):
    for side in range(2):
        for j in range(n_kv):
            for part in range(2):
                lanes = ((side * n_kv + j) * 2 + part) * LANES
                for block in range(kv_ref.shape[0] // BLK):
                    for rg in range(BLK // PIECE):
                        at = block * BLK + rg * PIECE
                        out_ref[(rg * 2 + part) * 2 + side, block * n_kv + j] = kv_ref[
                            at:at + PIECE, lanes:lanes + LANES
                        ]


def split_rows(kv_rows, n_kv):
    n_blk = kv_rows.shape[0] // BLK
    return pl.pallas_call(
        functools.partial(split_kernel, n_kv),
        in_specs=[pl.BlockSpec(memory_space=pltpu.VMEM)],
        out_specs=pl.BlockSpec(memory_space=pltpu.VMEM),
        out_shape=jax.ShapeDtypeStruct((2 * N_PIECES, n_blk * n_kv, PIECE, LANES), kv_rows.dtype),
        compiler_params=pltpu.CompilerParams(vmem_limit_bytes=ALL_VMEM),
    )(kv_rows)


def select_kernel(n_kv, n_vert, index_ref, table, out):
    for j in range(n_kv):
        for unit in range(n_vert):
            rows = slice(unit * PIECE, (unit + 1) * PIECE)
            out[j, rows, :] = table[index_ref[j * n_vert + unit]]


def select_units(index, table, n_kv, n_vert):
    return pl.pallas_call(
        functools.partial(select_kernel, n_kv, n_vert),
        in_specs=[
            pl.BlockSpec(memory_space=pltpu.SMEM),
            pl.BlockSpec(memory_space=pltpu.VMEM),
        ],
        out_specs=pl.BlockSpec(memory_space=pltpu.VMEM),
        out_shape=jax.ShapeDtypeStruct((n_kv, n_vert * PIECE, LANES), jnp.bfloat16),
        compiler_params=pltpu.CompilerParams(vmem_limit_bytes=8 * 1024 * 1024),
    )(index, table)


def assemble_kernel(widths, column_ref, *refs):
    n = len(widths)
    pieces, out, buffers, sem = refs[:n], refs[n], refs[n + 1:-1], refs[-1]
    loads = [pltpu.make_async_copy(pieces[i], buffers[i], sem.at[0, i]) for i in range(n)]
    start_all(loads)
    stores = []
    for i in range(n):
        loads[i].wait()
        start = pl.multiple_of(column_ref[i], LANES)
        stores.append(
            pltpu.make_async_copy(buffers[i], out.at[:, pl.ds(start, widths[i])], sem.at[1, i])
        )
        stores[-1].start()
    wait_all(stores)


def assemble(columns, pieces):
    rows = pieces[0].shape[0]
    widths = [piece.shape[1] for piece in pieces]
    return pl.pallas_call(
        functools.partial(assemble_kernel, widths),
        in_specs=[pl.BlockSpec(memory_space=pltpu.SMEM)] + [ANY] * len(pieces),
        out_specs=ANY,
        out_shape=jax.ShapeDtypeStruct((rows, sum(widths)), pieces[0].dtype),
        scratch_shapes=[pltpu.VMEM(piece.shape, piece.dtype) for piece in pieces]
        + [pltpu.SemaphoreType.DMA((2, len(pieces)))],
        compiler_params=pltpu.CompilerParams(vmem_limit_bytes=ALL_VMEM),
    )(columns, *pieces)


def mask_tables(vert, slash, first, n_query, n_win, n_vert, n_blocks):
    n_kv, group = vert.shape[:2]
    blocks = jnp.arange(n_blocks, dtype=jnp.int32)
    present = jnp.any(vert.reshape(n_kv, -1)[:, :, None] == blocks, axis=1)
    before = blocks[None, :] < blocks[:, None]
    rank = jnp.sum((present[:, None, :] & before[None]).astype(jnp.int32), axis=2)
    unit = jnp.arange(n_vert, dtype=jnp.int32)
    chosen = present[:, None, :] & (rank[:, None, :] == unit[None, :, None])
    units = jnp.sum(jnp.where(chosen, blocks, 0), axis=2)

    def as_rows(live):
        bias = jnp.where(live, 0.0, NEG).astype(jnp.bfloat16)
        bias = bias.reshape(n_kv, n_query * group, live.shape[-1])
        return jnp.pad(bias, ((0, 0), (0, 0), (0, LANES - live.shape[-1])))

    query = first + jnp.arange(n_query, dtype=jnp.int32)
    window = first - SMAX + jnp.arange(n_win, dtype=jnp.int32)
    offset = query[:, None] - window[None, :]
    by_slash = jnp.any(offset[None, :, None, :, None] == slash[:, None, :, None, :], axis=4)
    by_vert = jnp.any(window[None, None, :, None] == vert[:, :, None, :], axis=3)
    near = (offset >= 0) & (offset <= SMAX) & (window >= 0)[None, :]
    live_w = near[None, :, None, :] & (by_slash | by_vert[:, None, :, :])
    listed = jnp.any(units[:, None, :, None] == vert[:, :, None, :], axis=3)
    far = query[None, :, None] - units[:, None, :] > SMAX
    live_v = far[:, :, None, :] & listed[:, None, :, :]
    return units, as_rows(live_w), as_rows(live_v)


def paired(queries, kv_rows, vertical, slash):
    n_seq = lax.axis_size("seq")
    n_chip = n_seq // 2
    n_far = n_chip // 2
    tok = queries.shape[0]
    n_blk = tok // BLK
    seq_pos, tp_pos = lax.axis_index("seq"), lax.axis_index("tp")
    core, chip = seq_pos % 2, seq_pos // 2
    near, far = chip % 2, chip // 2
    heads_loc = vertical.shape[0] // 2
    kv_loc = kv_rows.shape[1] // (2 * HEAD_SIZE)
    group = heads_loc // kv_loc
    n_kv = kv_loc // 2
    heads = n_kv * group
    n_blocks = n_seq * n_blk
    n_vert = vertical.shape[1] * 3 // 2 - 1
    n_query = 2 * n_blk
    n_win = n_query + SMAX
    kv_width = n_kv * 2 * HEAD_SIZE
    q_width = heads * HEAD_SIZE

    def by_chip(array, target):
        pairs = []
        for source in range(n_seq):
            to = target(source // 2)
            if to is not None:
                pairs.append((source, 2 * to + source % 2))
        return lax.ppermute(array, "seq", pairs)

    to_pair = jnp.concatenate(
        [
            lax.dynamic_slice_in_dim(queries, (1 - core) * q_width, q_width, 1),
            lax.dynamic_slice_in_dim(kv_rows, (1 - core) * kv_width, kv_width, 1),
        ],
        axis=1,
    )
    from_pair = lax.ppermute(to_pair, "seq", [(i, i ^ 1) for i in range(n_seq)])

    rows, _ = lax.optimization_barrier((kv_rows, to_pair))
    held = lax.all_to_all(split_rows(rows, n_kv), "seq", split_axis=0, concat_axis=0, tiled=True)
    held = held.reshape(n_blocks * n_kv, PIECE, LANES)

    mine = lax.dynamic_slice_in_dim(kv_rows, core * kv_width, kv_width, 1)
    theirs = from_pair[:, q_width:]
    here = jnp.where(
        core == 0,
        jnp.concatenate([mine, theirs], axis=0),
        jnp.concatenate([theirs, mine], axis=0),
    )
    extra = SMAX - n_query
    tail = jnp.where(core == 0, theirs[-extra * BLK:], mine[-extra * BLK:])
    before = by_chip(here, lambda c: c + 1 if c + 1 < n_chip else None)
    back = by_chip(tail, lambda c: c + 2 if c + 2 < n_chip else None)

    vertical, slash, here, tail = lax.optimization_barrier((vertical, slash, here, tail))
    first_head = tp_pos * heads_loc + core * heads
    my_vert = lax.dynamic_slice_in_dim(vertical, first_head, heads, 0).reshape(n_kv, group, -1)
    my_slash = lax.dynamic_slice_in_dim(slash, first_head, heads, 0).reshape(n_kv, group, -1)
    units, bias_w, bias_v = mask_tables(
        my_vert, my_slash, chip * n_query, n_query, n_win, n_vert, n_blocks
    )

    index = (units * n_kv + jnp.arange(n_kv, dtype=jnp.int32)[:, None]).reshape(-1)
    picked = select_units(index, held, n_kv, n_vert)
    beside = by_chip(picked, lambda c: c ^ 1)
    both = jnp.where(near == 0, jnp.stack([picked, beside]), jnp.stack([beside, picked]))
    pieces, sources, slots = [both], [(0, 0), (0, 1)], [2 * far, 2 * far + 1]
    for step in range(1, n_far):
        pieces.append(by_chip(both, lambda c: (c + 2 * step) % n_chip))
        sources += [(step, 0), (step, 1)]
        owner = (far - step) % n_far
        slots += [2 * owner, 2 * owner + 1]

    pos = jnp.stack([core, tp_pos] + slots).astype(jnp.int32)
    state = window_part(
        pos, [here, before, back], [SMAX, extra, 0], bias_w, queries, from_pair,
        n_kv, 2, n_blk, group, n_win,
    )

    def swap(array, other_core, other_tp):
        pairs = []
        for source in range(n_seq):
            for t in range(2):
                pairs.append((source * 2 + t, (source ^ other_core) * 2 + (t ^ other_tp)))
        return lax.ppermute(array, ("seq", "tp"), pairs)

    results = []
    for other_tp, kvs in [(1, (j,)) for j in range(n_kv)] + [(0, tuple(range(n_kv)))]:
        outs = vertical_part(
            pos, pieces, sources, kvs, bias_v, queries, from_pair, state,
            n_kv, 2, 2, other_tp, n_blk, group, n_vert,
        )
        outs, state = lax.optimization_barrier((outs, state))
        from_tp = 1 - tp_pos if other_tp else tp_pos
        for other_core in (0, 1):
            from_core = 1 - core if other_core else core
            for m, j in enumerate(kvs):
                piece = outs[m * 2 + other_core]
                if other_core or other_tp:
                    piece = swap(piece, other_core, other_tp)
                column = ((from_tp * 2 + from_core) * n_kv + j) * group * HEAD_SIZE
                results.append((piece, column))
    columns = jnp.stack([column for _, column in results]).astype(jnp.int32)
    return assemble(columns, [piece for piece, _ in results])


def gathered(queries, kv_rows, vertical, slash):
    n_seq, n_tp = lax.axis_size("seq"), lax.axis_size("tp")
    tok = queries.shape[0]
    n_blk = tok // BLK
    seq_pos, tp_pos = lax.axis_index("seq"), lax.axis_index("tp")
    heads = vertical.shape[0] // n_tp
    n_kv = kv_rows.shape[1] // (2 * HEAD_SIZE)
    group = heads // n_kv
    n_blocks = n_seq * n_blk
    n_vert = vertical.shape[1] * 3 // 2 - 1
    n_win = n_blk + SMAX
    first = seq_pos * n_blk
    my_vert = lax.dynamic_slice_in_dim(vertical, tp_pos * heads, heads, 0)
    my_slash = lax.dynamic_slice_in_dim(slash, tp_pos * heads, heads, 0)
    units, bias_w, bias_v = mask_tables(
        my_vert.reshape(n_kv, group, -1), my_slash.reshape(n_kv, group, -1),
        first, n_blk, n_win, n_vert, n_blocks,
    )
    full = lax.all_gather(kv_rows, "seq", axis=0, tiled=True)
    padded = jnp.pad(full, ((SMAX * BLK, 0), (0, 0)))
    window = lax.dynamic_slice_in_dim(padded, first * BLK, n_win * BLK, 0)
    pos = jnp.stack([jnp.int32(0), tp_pos] + [jnp.int32(i) for i in range(N_PIECES)])
    state = window_part(
        pos, [window], [0], bias_w, queries, None, n_kv, 1, n_blk, group, n_win
    )
    blocks = full.reshape(n_blocks, BLK // PIECE, PIECE, n_kv, 2, LANES)
    listed = jnp.stack([blocks[units[j], :, :, j] for j in range(n_kv)])
    listed = jnp.transpose(listed, (2, 4, 0, 1, 3, 5))
    listed = listed.reshape(N_PIECES, n_kv, n_vert * PIECE, LANES)
    outs = vertical_part(
        pos, [listed], [(0, i) for i in range(N_PIECES)], tuple(range(n_kv)), bias_v, queries, None,
        state, n_kv, 1, 1, 0, n_blk, group, n_vert,
    )
    attended = jnp.concatenate(outs, axis=1)
    return lax.all_to_all(attended, "tp", split_axis=0, concat_axis=1, tiled=True)


def per_device(queries, kv_rows, vertical, slash):
    n_seq, n_tp = lax.axis_size("seq"), lax.axis_size("tp")
    kv_loc = kv_rows.shape[1] // (2 * HEAD_SIZE)
    n_blk = queries.shape[0] // BLK
    if n_seq == 2 * N_PIECES and n_tp == 2 and kv_loc % 2 == 0 and n_blk == 4:
        return paired(queries, kv_rows, vertical, slash)
    return gathered(queries, kv_rows, vertical, slash)


def solution(mesh):
    return jax.shard_map(
        per_device,
        mesh=mesh,
        in_specs=(P("seq", "tp"), P("seq", "tp"), P(), P()),
        out_specs=P(("seq", "tp"), None),
        check_vma=False,
    )
```

```python
import functools
import math

import jax
import jax.numpy as jnp
from jax import lax
from jax.experimental import pallas as pl
from jax.experimental.pallas import tpu as pltpu
from jax.sharding import PartitionSpec as P

HEAD_SIZE = 128
BLK = 64
SMAX = 11
PIECE = 16
N_PIECES = (BLK // PIECE) * 2
LANES = 128
NEG = -1e30
SCALE = math.log2(math.e) / math.sqrt(HEAD_SIZE)
LOG_SCALE = math.sqrt(HEAD_SIZE)
ANY = pl.BlockSpec(memory_space=pl.ANY)


VMEM_LIMIT = 32 * 1024 * 1024
ALL_VMEM = 60 * 1024 * 1024


def round_up(value, unit):
    return (value + unit - 1) // unit * unit


def head_rows(ref, block, group):
    rows = slice(block * BLK, (block + 1) * BLK)
    heads = [ref[rows, h * HEAD_SIZE:(h + 1) * HEAD_SIZE] for h in range(group)]
    return jnp.concatenate(heads, axis=0)


def with_selector(q, block, group):
    shape = (q.shape[0], LANES)
    wanted = lax.broadcasted_iota(jnp.int32, shape, 0) // BLK + block * group
    pick = lax.broadcasted_iota(jnp.int32, shape, 1) == wanted
    return jnp.concatenate([q, jnp.where(pick, 1.0, 0.0).astype(jnp.bfloat16)], axis=1)


def in_pipeline(count, scores_of, softmax_of, finish):
    scores = scores_of(0)
    waiting = None
    for n in range(count):
        following = scores_of(n + 1) if n + 1 < count else None
        current = softmax_of(n, scores)
        if waiting is not None:
            finish(*waiting)
        waiting = (n, *current)
        scores = following
    finish(*waiting)


def tiles(array):
    return [array[:, at:at + LANES] for at in range(0, array.shape[1], LANES)]


def row_top(parts):
    top = functools.reduce(jnp.maximum, parts)
    return jnp.broadcast_to(jnp.max(top, axis=1, keepdims=True), top.shape)


def exponents(parts, top):
    return jnp.concatenate(
        [jnp.exp2((part - top) * SCALE).astype(jnp.bfloat16) for part in parts], axis=1
    )


def start_all(copies):
    for copy in copies:
        copy.start()


def wait_all(copies):
    for copy in copies:
        copy.wait()


def spread_mask(table, block_of_key, n_keys):
    shape = (LANES, n_keys)
    key = lax.broadcasted_iota(jnp.int32, shape, 1)
    own = lax.broadcasted_iota(jnp.int32, shape, 0) == block_of_key(key)
    own = jnp.where(own, 1.0, 0.0).astype(jnp.bfloat16)
    return jnp.dot(table, own, preferred_element_type=jnp.float32).astype(jnp.bfloat16)


def window_kernel(sizes, places, kvs, n_kv, n_src, n_blk, group, pos_ref, *refs):
    n_mine = len(kvs)
    n_pieces = len(sizes)
    pieces, refs = refs[:n_pieces], refs[n_pieces:]
    bias_ref, refs = refs[0], refs[1:]
    q_in, refs = refs[:n_src], refs[n_src:]
    acc_out, lse_out, table, mask, kaug, vaug, q_ref, acc_ref, lse_ref, sem, turn_sem = refs
    core = pos_ref[0]
    n_rows = table.shape[1]
    n_lanes = kaug.shape[3]
    n_mask = bias_ref.shape[1]
    width = group * HEAD_SIZE
    span = (SMAX + 1) * BLK
    rows = group * BLK
    tok = n_blk * BLK
    n_pairs = n_src * n_blk // 2
    count = iter(range(sem.shape[0]))

    loads = []
    for m, j in enumerate(kvs):
        mine = []
        lanes = pl.ds(j * 2 * HEAD_SIZE, 2 * HEAD_SIZE)
        for index in range(n_pieces):
            at = pl.ds(places[index] * BLK, sizes[index])
            mine.append((pieces[index].at[:, lanes], table.at[m, at]))
        mine.append((bias_ref.at[j], mask.at[m]))
        first = pl.multiple_of((core * n_kv + j) * width, width)
        q_lanes = [pl.ds(first, width), pl.ds(j * width, width)]
        for source in range(n_src):
            at = pl.ds((m * n_src + source) * tok, tok)
            mine.append((q_in[source].at[:, q_lanes[source]], q_ref.at[at]))
        loads.append([pltpu.make_async_copy(*pair, sem.at[next(count)]) for pair in mine])
    for mine in loads:
        start_all(mine)
    for m in range(n_mine):
        vaug[m, :, HEAD_SIZE:] = jnp.ones((n_rows, LANES), jnp.bfloat16)
        for odd in range(2):
            kaug[m, odd, HEAD_SIZE + n_mask:, :] = jnp.zeros((LANES - n_mask, n_lanes), jnp.bfloat16)
    for m in range(n_mine):
        wait_all(loads[m])
        for odd in range(2):
            kaug[m, odd, :HEAD_SIZE, :] = table[m, odd * BLK:odd * BLK + n_lanes, :HEAD_SIZE].T
            kaug[m, odd, HEAD_SIZE:HEAD_SIZE + n_mask, :] = spread_mask(
                mask[m], lambda key: key // BLK + odd, n_lanes
            )
        vaug[m, :, :HEAD_SIZE] = table[m, :, HEAD_SIZE:]

    u = lax.broadcasted_iota(jnp.int32, (rows, LANES), 1) - (LANES - BLK)
    t = lax.broadcasted_iota(jnp.int32, (rows, LANES), 0) % BLK

    def stores(turn):
        blocks = pl.ds(2 * turn, 2)
        return [
            pltpu.make_async_copy(acc_ref.at[blocks], acc_out.at[blocks], turn_sem.at[turn, 0]),
            pltpu.make_async_copy(lse_ref.at[blocks], lse_out.at[blocks], turn_sem.at[turn, 1]),
        ]

    def two_blocks(turn, carry):
        m, pair = turn // n_pairs, turn % n_pairs
        base = 2 * pair
        if n_src == 2:
            per = n_blk // 2
            base = jnp.where(pair < per, core, 1 - core) * n_blk + 2 * (pair % per)
        q_rows = q_ref.at[pl.ds(pl.multiple_of(2 * turn * BLK, 2 * BLK), 2 * BLK)]
        even = pl.ds(pl.multiple_of(base * BLK, LANES), span)

        def scores_of(n):
            q = with_selector(head_rows(q_rows, n, group), base + n, group)
            return jnp.dot(q, kaug[m, n, :, even], preferred_element_type=jnp.float32)

        def softmax_of(n, scores):
            parts = tiles(scores)
            parts[-1] = jnp.where(u > t, NEG, parts[-1])
            top = row_top(parts)
            return top, exponents(parts, top)

        def finish(n, top, weights):
            at = pl.ds(pl.multiple_of((base + n) * BLK, BLK), span)
            total = jnp.dot(weights, vaug[m, at, :], preferred_element_type=jnp.float32)
            acc_ref[2 * turn + n] = total[:, :HEAD_SIZE] / total[:, HEAD_SIZE:]
            lse_ref[2 * turn + n] = top + jnp.log(total[:, HEAD_SIZE:]) * LOG_SCALE

        in_pipeline(2, scores_of, softmax_of, finish)
        start_all(stores(turn))
        return carry

    lax.fori_loop(0, n_mine * n_pairs, two_blocks, 0)
    for turn in range(n_mine * n_pairs):
        wait_all(stores(turn))


def window_part(pos, pieces, places, kvs, bias, queries, q_recv, n_kv, n_src, n_blk, group, n_win):
    n_mine = len(kvs)
    width = group * HEAD_SIZE
    rows = group * BLK
    n_rows = n_win * BLK
    n_turns = n_mine * n_src * n_blk // 2
    q_args = [queries] if n_src == 1 else [queries, q_recv]
    out_shape = jax.ShapeDtypeStruct((2 * n_turns, rows, LANES), jnp.float32)
    sizes = [piece.shape[0] for piece in pieces]
    keys = 2 * n_turns * rows * (SMAX + 1) * BLK
    return pl.pallas_call(
        functools.partial(window_kernel, sizes, places, kvs, n_kv, n_src, n_blk, group),
        in_specs=[pl.BlockSpec(memory_space=pltpu.SMEM)]
        + [ANY] * (len(pieces) + 1 + n_src),
        out_specs=[ANY, ANY],
        scratch_shapes=[
            pltpu.VMEM((n_mine, n_rows, 2 * HEAD_SIZE), jnp.bfloat16),
            pltpu.VMEM((n_mine,) + bias.shape[1:], jnp.bfloat16),
            pltpu.VMEM((n_mine, 2, 2 * LANES, n_rows - BLK), jnp.bfloat16),
            pltpu.VMEM((n_mine, n_rows, 2 * LANES), jnp.bfloat16),
            pltpu.VMEM((2 * n_turns * BLK, width), jnp.bfloat16),
            pltpu.VMEM(out_shape.shape, jnp.float32),
            pltpu.VMEM(out_shape.shape, jnp.float32),
            pltpu.SemaphoreType.DMA((n_mine * (len(pieces) + 1 + n_src),)),
            pltpu.SemaphoreType.DMA((n_turns, 2)),
        ],
        out_shape=[out_shape, out_shape],
        compiler_params=pltpu.CompilerParams(vmem_limit_bytes=VMEM_LIMIT),
        cost_estimate=pl.CostEstimate(
            flops=keys * 1024, bytes_accessed=16 * 1024 * 1024, transcendentals=keys
        ),
    )(pos, *pieces, bias, *q_args)


def vertical_kernel(sources, kvs, n_kv, n_vert, group, n_blk, n_src, n_dst, other, direct, pos_ref, *refs):
    n_pieces = max(source[0] for source in sources) + 1
    n_mine = len(kvs)
    pieces, refs = refs[:n_pieces], refs[n_pieces:]
    bias_ref, refs = refs[0], refs[1:]
    q_in, refs = refs[:n_src], refs[n_src:]
    states_in, refs = refs[:2], refs[2:]
    n_outs = 1 + n_mine * (n_src - 1) if direct else n_mine * n_src
    outs_ref, refs = refs[:n_outs], refs[n_outs:]
    table, mask, kaug, vaug, q_ref, acc_ref, lse_ref, out_ref, sem, turn_sem = refs
    core, tp_pos = pos_ref[0], pos_ref[1]
    per_dst = n_blk // n_dst
    n_keys = vaug.shape[1]
    n_mask = bias_ref.shape[1]
    group_rows = n_vert * PIECE
    used = (N_PIECES // 2) * group_rows
    width = group * HEAD_SIZE
    base = 0
    if n_dst > 1:
        base = (1 - tp_pos if other else tp_pos) * per_dst
    count = iter(range(sem.shape[0]))

    loads = []
    for m, j in enumerate(kvs):
        for index, (piece, part) in enumerate(sources):
            slot = pos_ref[2 + index]
            rows = pl.ds(pl.multiple_of((slot // 2) * group_rows, PIECE), group_rows)
            loads.append(
                pltpu.make_async_copy(
                    pieces[piece].at[part, j], table.at[m, slot % 2, rows], sem.at[next(count)]
                )
            )
        loads.append(pltpu.make_async_copy(bias_ref.at[j], mask.at[m], sem.at[next(count)]))
    q_rows = pl.ds(pl.multiple_of(base * BLK, BLK), per_dst * BLK)

    def turn_loads(m, source, turn):
        j = kvs[m]
        first = pl.multiple_of((core * n_kv + j) * width, width)
        q_lanes = [pl.ds(first, width), pl.ds(j * width, width)]
        blocks = pl.ds((j * n_src + source) * n_blk + base, per_dst)
        return [
            pltpu.make_async_copy(
                q_in[source].at[q_rows, q_lanes[source]], q_ref.at[turn], turn_sem.at[turn, 0]
            ),
            pltpu.make_async_copy(
                states_in[0].at[blocks], acc_ref.at[turn], turn_sem.at[turn, 1]
            ),
            pltpu.make_async_copy(
                states_in[1].at[blocks], lse_ref.at[turn], turn_sem.at[turn, 2]
            ),
        ]

    start_all(loads)
    for m in range(n_mine):
        for source in range(n_src):
            start_all(turn_loads(m, source, m * n_src + source))
    for m in range(n_mine):
        if used < n_keys:
            empty = jnp.zeros((n_keys - used, LANES), jnp.bfloat16)
            table[m, 0, used:] = empty
            table[m, 1, used:] = empty
        vaug[m, :, HEAD_SIZE:] = jnp.ones((n_keys, LANES), jnp.bfloat16)
        kaug[m, HEAD_SIZE + n_mask:, :] = jnp.zeros((LANES - n_mask, n_keys), jnp.bfloat16)
    wait_all(loads)
    for m in range(n_mine):
        kaug[m, :HEAD_SIZE, :] = table[m, 0].T
        kaug[m, HEAD_SIZE:HEAD_SIZE + n_mask, :] = spread_mask(
            mask[m], lambda key: key % group_rows // PIECE, n_keys
        )
        if used < n_keys:
            kaug[m, HEAD_SIZE:HEAD_SIZE + n_mask, used:] = jnp.full((n_mask, n_keys - used), NEG, jnp.bfloat16)
        vaug[m, :, :HEAD_SIZE] = table[m, 1]

    def one_turn(turn, carry):
        j = turn // n_src
        first_block = base
        if n_src == 2:
            first_block = base + jnp.where(turn % 2 == 0, core, 1 - core) * n_blk
        wait_all(turn_loads(0, 0, turn))

        def scores_of(n):
            q = with_selector(head_rows(q_ref.at[turn], n, group), first_block + n, group)
            return jnp.dot(q, kaug[j], preferred_element_type=jnp.float32)

        def softmax_of(n, scores):
            old = lse_ref[turn, n]
            parts = tiles(scores)
            top = jnp.maximum(old, row_top(parts))
            return jnp.exp2((old - top) * SCALE), exponents(parts, top)

        def finish(n, shrink, weights):
            total = jnp.dot(weights, vaug[j], preferred_element_type=jnp.float32)
            weighted = total[:, :HEAD_SIZE] + acc_ref[turn, n] * shrink
            out = (weighted / (total[:, HEAD_SIZE:] + shrink)).astype(jnp.bfloat16)
            for h in range(group):
                lanes = slice(h * HEAD_SIZE, (h + 1) * HEAD_SIZE)
                out_ref[turn, n * BLK:(n + 1) * BLK, lanes] = out[h * BLK:(h + 1) * BLK]

        in_pipeline(per_dst, scores_of, softmax_of, finish)
        return carry

    lax.fori_loop(0, n_mine * n_src, one_turn, 0)
    stores = []
    for m in range(n_mine):
        for source in range(n_src):
            turn = m * n_src + source
            if direct and source == 0:
                column = pl.multiple_of(((tp_pos * n_src + core) * n_kv + kvs[m]) * width, width)
                target = outs_ref[0].at[:, pl.ds(column, width)]
            elif direct:
                target = outs_ref[1 + m]
            else:
                target = outs_ref[turn]
            stores.append(pltpu.make_async_copy(out_ref.at[turn], target, turn_sem.at[turn, 3]))
    start_all(stores)
    wait_all(stores)


def vertical_part(
    pos, pieces, sources, kvs, bias, queries, q_recv, states,
    n_kv, n_src, n_dst, other, direct, n_blk, group, n_vert,
):
    n_mine = len(kvs)
    n_turns = n_mine * n_src
    width = group * HEAD_SIZE
    rows = group * BLK
    per_dst = n_blk // n_dst
    n_keys = round_up(n_vert * BLK, LANES)
    q_args = [queries] if n_src == 1 else [queries, q_recv]
    piece = jax.ShapeDtypeStruct((per_dst * BLK, width), jnp.bfloat16)
    out_shapes = [piece] * n_turns
    if direct:
        whole = (per_dst * BLK, width * n_kv * n_src * n_dst)
        out_shapes = [jax.ShapeDtypeStruct(whole, jnp.bfloat16)] + [piece] * (n_mine * (n_src - 1))
    keys = n_turns * per_dst * rows * n_keys
    args = [*pieces, bias, *q_args, *states]
    return pl.pallas_call(
        functools.partial(
            vertical_kernel, sources, kvs, n_kv, n_vert, group, n_blk, n_src, n_dst, other, direct
        ),
        in_specs=[pl.BlockSpec(memory_space=pltpu.SMEM)] + [ANY] * len(args),
        out_specs=[ANY] * len(out_shapes),
        scratch_shapes=[
            pltpu.VMEM((n_mine, 2, n_keys, LANES), jnp.bfloat16),
            pltpu.VMEM((n_mine,) + bias.shape[1:], jnp.bfloat16),
            pltpu.VMEM((n_mine, 2 * LANES, n_keys), jnp.bfloat16),
            pltpu.VMEM((n_mine, n_keys, 2 * LANES), jnp.bfloat16),
            pltpu.VMEM((n_turns, per_dst * BLK, width), jnp.bfloat16),
            pltpu.VMEM((n_turns, per_dst, rows, LANES), jnp.float32),
            pltpu.VMEM((n_turns, per_dst, rows, LANES), jnp.float32),
            pltpu.VMEM((n_turns, per_dst * BLK, width), jnp.bfloat16),
            pltpu.SemaphoreType.DMA((n_mine * (N_PIECES + 1),)),
            pltpu.SemaphoreType.DMA((n_turns, 4)),
        ],
        out_shape=out_shapes,
        compiler_params=pltpu.CompilerParams(vmem_limit_bytes=(16 + round_up(8 * n_keys // 768, 8)) * 1024 * 1024),
        cost_estimate=pl.CostEstimate(
            flops=keys * 1024, bytes_accessed=8 * 1024 * 1024, transcendentals=keys
        ),
    )(pos, *args)


def split_kernel(n_kv, kv_ref, out_ref):
    for side in range(2):
        for j in range(n_kv):
            for part in range(2):
                lanes = ((side * n_kv + j) * 2 + part) * LANES
                for block in range(kv_ref.shape[0] // BLK):
                    for rg in range(BLK // PIECE):
                        at = block * BLK + rg * PIECE
                        out_ref[(rg * 2 + part) * 2 + side, block * n_kv + j] = kv_ref[
                            at:at + PIECE, lanes:lanes + LANES
                        ]


def split_rows(kv_rows, n_kv):
    n_blk = kv_rows.shape[0] // BLK
    return pl.pallas_call(
        functools.partial(split_kernel, n_kv),
        in_specs=[pl.BlockSpec(memory_space=pltpu.VMEM)],
        out_specs=pl.BlockSpec(memory_space=pltpu.VMEM),
        out_shape=jax.ShapeDtypeStruct((2 * N_PIECES, n_blk * n_kv, PIECE, LANES), kv_rows.dtype),
        compiler_params=pltpu.CompilerParams(vmem_limit_bytes=ALL_VMEM),
    )(kv_rows)


def select_kernel(n_kv, n_vert, index_ref, table, out):
    for j in range(n_kv):
        for unit in range(n_vert):
            rows = slice(unit * PIECE, (unit + 1) * PIECE)
            out[j, rows, :] = table[index_ref[j * n_vert + unit]]


def select_units(index, table, n_kv, n_vert):
    return pl.pallas_call(
        functools.partial(select_kernel, n_kv, n_vert),
        in_specs=[
            pl.BlockSpec(memory_space=pltpu.SMEM),
            pl.BlockSpec(memory_space=pltpu.VMEM),
        ],
        out_specs=pl.BlockSpec(memory_space=pltpu.VMEM),
        out_shape=jax.ShapeDtypeStruct((n_kv, n_vert * PIECE, LANES), jnp.bfloat16),
        compiler_params=pltpu.CompilerParams(vmem_limit_bytes=8 * 1024 * 1024),
    )(index, table)


def assemble_kernel(n, column_ref, *refs):
    pieces, (_, out), buffers, sem = refs[:n], refs[n:n + 2], refs[n + 2:-1], refs[-1]
    loads = [pltpu.make_async_copy(pieces[i], buffers[i], sem.at[0, i]) for i in range(n)]
    start_all(loads)
    stores = []
    for i in range(n):
        loads[i].wait()
        width = buffers[i].shape[1]
        start = pl.multiple_of(column_ref[i], width)
        stores.append(
            pltpu.make_async_copy(buffers[i], out.at[:, pl.ds(start, width)], sem.at[1, i])
        )
        stores[-1].start()
    wait_all(stores)


def assemble(out, results, vmem):
    pieces = [piece for piece, _ in results]
    columns = jnp.stack([column for _, column in results]).astype(jnp.int32)
    n = len(pieces)
    return pl.pallas_call(
        functools.partial(assemble_kernel, n),
        in_specs=[pl.BlockSpec(memory_space=pltpu.SMEM)] + [ANY] * (n + 1),
        out_specs=ANY,
        out_shape=jax.ShapeDtypeStruct(out.shape, out.dtype),
        scratch_shapes=[pltpu.VMEM(piece.shape, piece.dtype) for piece in pieces]
        + [pltpu.SemaphoreType.DMA((2, n))],
        input_output_aliases={n + 1: 0},
        compiler_params=pltpu.CompilerParams(vmem_limit_bytes=vmem),
    )(columns, *pieces, out)


def mask_tables(vert, slash, first, n_query, n_win, n_vert, n_blocks):
    n_kv, group = vert.shape[:2]
    blocks = jnp.arange(n_blocks, dtype=jnp.int32)
    present = jnp.any(vert.reshape(n_kv, -1)[:, :, None] == blocks, axis=1)
    before = blocks[None, :] < blocks[:, None]
    rank = jnp.sum((present[:, None, :] & before[None]).astype(jnp.int32), axis=2)
    unit = jnp.arange(n_vert, dtype=jnp.int32)
    chosen = present[:, None, :] & (rank[:, None, :] == unit[None, :, None])
    units = jnp.sum(jnp.where(chosen, blocks, 0), axis=2)

    def as_rows(live):
        bias = jnp.where(live, 0.0, NEG).astype(jnp.bfloat16)
        bias = bias.reshape(n_kv, n_query * group, live.shape[-1])
        return jnp.pad(bias, ((0, 0), (0, 0), (0, LANES - live.shape[-1])))

    query = first + jnp.arange(n_query, dtype=jnp.int32)
    window = first - SMAX + jnp.arange(n_win, dtype=jnp.int32)
    offset = query[:, None] - window[None, :]
    by_slash = jnp.any(offset[None, :, None, :, None] == slash[:, None, :, None, :], axis=4)
    by_vert = jnp.any(window[None, None, :, None] == vert[:, :, None, :], axis=3)
    near = (offset >= 0) & (offset <= SMAX) & (window >= 0)[None, :]
    live_w = near[None, :, None, :] & (by_slash | by_vert[:, None, :, :])
    listed = jnp.any(units[:, None, :, None] == vert[:, :, None, :], axis=3)
    far = query[None, :, None] - units[:, None, :] > SMAX
    live_v = far[:, :, None, :] & listed[:, None, :, :]
    return units, as_rows(live_w), as_rows(live_v)


def paired(queries, kv_rows, vertical, slash):
    n_seq = lax.axis_size("seq")
    n_chip = n_seq // 2
    n_far = n_chip // 2
    tok = queries.shape[0]
    n_blk = tok // BLK
    seq_pos, tp_pos = lax.axis_index("seq"), lax.axis_index("tp")
    core, chip = seq_pos % 2, seq_pos // 2
    near, far = chip % 2, chip // 2
    heads_loc = vertical.shape[0] // 2
    kv_loc = kv_rows.shape[1] // (2 * HEAD_SIZE)
    group = heads_loc // kv_loc
    n_kv = kv_loc // 2
    heads = n_kv * group
    n_blocks = n_seq * n_blk
    n_vert = vertical.shape[1] * 3 // 2 - 1
    n_query = 2 * n_blk
    n_win = n_query + SMAX
    kv_width = n_kv * 2 * HEAD_SIZE
    q_width = heads * HEAD_SIZE

    def by_chip(array, target):
        pairs = []
        for source in range(n_seq):
            to = target(source // 2)
            if to is not None:
                pairs.append((source, 2 * to + source % 2))
        return lax.ppermute(array, "seq", pairs)

    pair = [(i, i ^ 1) for i in range(n_seq)]
    kv_other = lax.dynamic_slice_in_dim(kv_rows, (1 - core) * kv_width, kv_width, 1)
    theirs = lax.ppermute(kv_other, "seq", pair)

    rows, _ = lax.optimization_barrier((kv_rows, kv_other))
    held = lax.all_to_all(split_rows(rows, n_kv), "seq", split_axis=0, concat_axis=0, tiled=True)
    held = held.reshape(n_blocks * n_kv, PIECE, LANES)

    mine = lax.dynamic_slice_in_dim(kv_rows, core * kv_width, kv_width, 1)
    here = jnp.where(
        core == 0,
        jnp.concatenate([mine, theirs], axis=0),
        jnp.concatenate([theirs, mine], axis=0),
    )
    extra = SMAX - n_query
    tail = jnp.where(core == 0, theirs[-extra * BLK:], mine[-extra * BLK:])
    before = by_chip(here, lambda c: c + 1 if c + 1 < n_chip else None)
    back = by_chip(tail, lambda c: c + 2 if c + 2 < n_chip else None)

    q_rows, here, tail = lax.optimization_barrier((queries, here, tail))
    q_other = lax.dynamic_slice_in_dim(q_rows, (1 - core) * q_width, q_width, 1)
    from_pair = lax.ppermute(q_other, "seq", pair)

    first_head = tp_pos * heads_loc + core * heads
    my_vert = lax.dynamic_slice_in_dim(vertical, first_head, heads, 0).reshape(n_kv, group, -1)
    my_slash = lax.dynamic_slice_in_dim(slash, first_head, heads, 0).reshape(n_kv, group, -1)
    units, bias_w, bias_v = mask_tables(
        my_vert, my_slash, chip * n_query, n_query, n_win, n_vert, n_blocks
    )

    index = (units * n_kv + jnp.arange(n_kv, dtype=jnp.int32)[:, None]).reshape(-1)
    picked = select_units(index, held, n_kv, n_vert)
    picked, from_pair = lax.optimization_barrier((picked, from_pair))
    beside = by_chip(picked, lambda c: c ^ 1)
    both = jnp.where(near == 0, jnp.stack([picked, beside]), jnp.stack([beside, picked]))
    pieces, sources, slots = [both], [(0, 0), (0, 1)], [2 * far, 2 * far + 1]
    for step in range(1, n_far):
        pieces.append(by_chip(both, lambda c: (c + 2 * step) % n_chip))
        sources += [(step, 0), (step, 1)]
        owner = (far - step) % n_far
        slots += [2 * owner, 2 * owner + 1]

    pos = jnp.stack([core, tp_pos] + slots).astype(jnp.int32)
    states = window_part(
        pos, [here, back, before], [SMAX, 0, extra], tuple(range(n_kv)), bias_w, queries, from_pair,
        n_kv, 2, n_blk, group, n_win,
    )

    def swap(array, other_core, other_tp):
        pairs = []
        for source in range(n_seq):
            for t in range(2):
                pairs.append((source * 2 + t, (source ^ other_core) * 2 + (t ^ other_tp)))
        return lax.ppermute(array, ("seq", "tp"), pairs)

    results = []
    for other_tp, kvs in [(1, (j,)) for j in range(n_kv)] + [(0, tuple(range(n_kv)))]:
        outs = vertical_part(
            pos, pieces, sources, kvs, bias_v, queries, from_pair, states,
            n_kv, 2, 2, other_tp, not other_tp, n_blk, group, n_vert,
        )
        outs, states = lax.optimization_barrier((outs, states))
        from_tp = 1 - tp_pos if other_tp else tp_pos
        if not other_tp:
            out, *outs = outs
        cores = (0, 1) if other_tp else (1,)
        turns = [(j, other_core) for j in kvs for other_core in cores]
        for (j, other_core), piece in zip(turns, outs, strict=True):
            from_core = 1 - core if other_core else core
            column = ((from_tp * 2 + from_core) * n_kv + j) * group * HEAD_SIZE
            results.append((swap(piece, other_core, other_tp), column))
    early = 2 * (n_kv - 1)
    return assemble(assemble(out, results[:early], ALL_VMEM), results[early:], VMEM_LIMIT // 4)


def gathered(queries, kv_rows, vertical, slash):
    n_seq, n_tp = lax.axis_size("seq"), lax.axis_size("tp")
    tok = queries.shape[0]
    n_blk = tok // BLK
    seq_pos, tp_pos = lax.axis_index("seq"), lax.axis_index("tp")
    heads = vertical.shape[0] // n_tp
    n_kv = kv_rows.shape[1] // (2 * HEAD_SIZE)
    group = heads // n_kv
    n_blocks = n_seq * n_blk
    n_vert = vertical.shape[1] * 3 // 2 - 1
    n_win = n_blk + SMAX
    first = seq_pos * n_blk
    my_vert = lax.dynamic_slice_in_dim(vertical, tp_pos * heads, heads, 0)
    my_slash = lax.dynamic_slice_in_dim(slash, tp_pos * heads, heads, 0)
    units, bias_w, bias_v = mask_tables(
        my_vert.reshape(n_kv, group, -1), my_slash.reshape(n_kv, group, -1),
        first, n_blk, n_win, n_vert, n_blocks,
    )
    full = lax.all_gather(kv_rows, "seq", axis=0, tiled=True)
    padded = jnp.pad(full, ((SMAX * BLK, 0), (0, 0)))
    window = lax.dynamic_slice_in_dim(padded, first * BLK, n_win * BLK, 0)
    pos = jnp.stack([jnp.int32(0), tp_pos] + [jnp.int32(i) for i in range(N_PIECES)])
    states = window_part(
        pos, [window], [0], tuple(range(n_kv)), bias_w, queries, None, n_kv, 1, n_blk, group, n_win
    )
    blocks = full.reshape(n_blocks, BLK // PIECE, PIECE, n_kv, 2, LANES)
    listed = jnp.stack([blocks[units[j], :, :, j] for j in range(n_kv)])
    listed = jnp.transpose(listed, (2, 4, 0, 1, 3, 5))
    listed = listed.reshape(N_PIECES, n_kv, n_vert * PIECE, LANES)
    outs = vertical_part(
        pos, [listed], [(0, i) for i in range(N_PIECES)], tuple(range(n_kv)), bias_v, queries, None,
        states, n_kv, 1, 1, 0, True, n_blk, group, n_vert,
    )
    attended = outs[0]
    return lax.all_to_all(attended, "tp", split_axis=0, concat_axis=1, tiled=True)


def per_device(queries, kv_rows, vertical, slash):
    n_seq, n_tp = lax.axis_size("seq"), lax.axis_size("tp")
    kv_loc = kv_rows.shape[1] // (2 * HEAD_SIZE)
    n_blk = queries.shape[0] // BLK
    if n_seq == 2 * N_PIECES and n_tp == 2 and kv_loc % 2 == 0 and n_blk == 4:
        return paired(queries, kv_rows, vertical, slash)
    return gathered(queries, kv_rows, vertical, slash)


def solution(mesh):
    return jax.shard_map(
        per_device,
        mesh=mesh,
        in_specs=(P("seq", "tp"), P("seq", "tp"), P(), P()),
        out_specs=P(("seq", "tp"), None),
        check_vma=False,
    )
```

```python
import functools
import math

import jax
import jax.numpy as jnp
from jax import lax
from jax.experimental import pallas as pl
from jax.experimental.pallas import tpu as pltpu
from jax.sharding import PartitionSpec as P

HEAD_SIZE = 128
BLK = 64
SMAX = 11
PIECE = 16
N_PIECES = (BLK // PIECE) * 2
LANES = 128
NEG = -1e30
SCALE = math.log2(math.e) / math.sqrt(HEAD_SIZE)
LOG_SCALE = math.sqrt(HEAD_SIZE)
ANY = pl.BlockSpec(memory_space=pl.ANY)


VMEM_LIMIT = 32 * 1024 * 1024
ALL_VMEM = 60 * 1024 * 1024


def round_up(value, unit):
    return (value + unit - 1) // unit * unit


def head_rows(ref, block, group):
    rows = slice(block * BLK, (block + 1) * BLK)
    heads = [ref[rows, h * HEAD_SIZE:(h + 1) * HEAD_SIZE] for h in range(group)]
    return jnp.concatenate(heads, axis=0)


def with_selector(q, block, group):
    shape = (q.shape[0], LANES)
    wanted = lax.broadcasted_iota(jnp.int32, shape, 0) // BLK + block * group
    pick = lax.broadcasted_iota(jnp.int32, shape, 1) == wanted
    return jnp.concatenate([q, jnp.where(pick, 1.0, 0.0).astype(jnp.bfloat16)], axis=1)


def in_pipeline(count, scores_of, softmax_of, finish):
    scores = scores_of(0)
    waiting = None
    for n in range(count):
        following = scores_of(n + 1) if n + 1 < count else None
        current = softmax_of(n, scores)
        if waiting is not None:
            finish(*waiting)
        waiting = (n, *current)
        scores = following
    finish(*waiting)


def tiles(array):
    return [array[:, at:at + LANES] for at in range(0, array.shape[1], LANES)]


def row_top(parts):
    top = functools.reduce(jnp.maximum, parts)
    return jnp.broadcast_to(jnp.max(top, axis=1, keepdims=True), top.shape)


def exponents(parts, top):
    return jnp.concatenate(
        [jnp.exp2((part - top) * SCALE).astype(jnp.bfloat16) for part in parts], axis=1
    )


def start_all(copies):
    for copy in copies:
        copy.start()


def wait_all(copies):
    for copy in copies:
        copy.wait()


def spread_mask(table, block_of_key, n_keys):
    shape = (LANES, n_keys)
    key = lax.broadcasted_iota(jnp.int32, shape, 1)
    own = lax.broadcasted_iota(jnp.int32, shape, 0) == block_of_key(key)
    own = jnp.where(own, 1.0, 0.0).astype(jnp.bfloat16)
    return jnp.dot(table, own, preferred_element_type=jnp.float32).astype(jnp.bfloat16)


def window_kernel(sizes, places, kvs, n_kv, n_src, n_blk, group, pos_ref, *refs):
    n_mine = len(kvs)
    n_pieces = len(sizes)
    pieces, refs = refs[:n_pieces], refs[n_pieces:]
    bias_ref, refs = refs[0], refs[1:]
    q_in, refs = refs[:n_src], refs[n_src:]
    acc_out, lse_out, table, mask, kaug, vaug, q_ref, acc_ref, lse_ref, sem, turn_sem = refs
    core = pos_ref[0]
    n_rows = table.shape[1]
    n_lanes = kaug.shape[3]
    n_mask = bias_ref.shape[1]
    width = group * HEAD_SIZE
    span = (SMAX + 1) * BLK
    rows = group * BLK
    tok = n_blk * BLK
    n_pairs = n_src * n_blk // 2
    count = iter(range(sem.shape[0]))

    loads = []
    for m, j in enumerate(kvs):
        mine = []
        lanes = pl.ds(j * 2 * HEAD_SIZE, 2 * HEAD_SIZE)
        for index in range(n_pieces):
            at = pl.ds(places[index] * BLK, sizes[index])
            mine.append((pieces[index].at[:, lanes], table.at[m, at]))
        mine.append((bias_ref.at[j], mask.at[m]))
        first = pl.multiple_of((core * n_kv + j) * width, width)
        q_lanes = [pl.ds(first, width), pl.ds(j * width, width)]
        for source in range(n_src):
            at = pl.ds((m * n_src + source) * tok, tok)
            mine.append((q_in[source].at[:, q_lanes[source]], q_ref.at[at]))
        loads.append([pltpu.make_async_copy(*pair, sem.at[next(count)]) for pair in mine])
    for mine in loads:
        start_all(mine)
    for m in range(n_mine):
        vaug[m, :, HEAD_SIZE:] = jnp.ones((n_rows, LANES), jnp.bfloat16)
        for odd in range(2):
            kaug[m, odd, HEAD_SIZE + n_mask:, :] = jnp.zeros((LANES - n_mask, n_lanes), jnp.bfloat16)
    for m in range(n_mine):
        wait_all(loads[m])
        for odd in range(2):
            kaug[m, odd, :HEAD_SIZE, :] = table[m, odd * BLK:odd * BLK + n_lanes, :HEAD_SIZE].T
            kaug[m, odd, HEAD_SIZE:HEAD_SIZE + n_mask, :] = spread_mask(
                mask[m], lambda key: key // BLK + odd, n_lanes
            )
        vaug[m, :, :HEAD_SIZE] = table[m, :, HEAD_SIZE:]

    u = lax.broadcasted_iota(jnp.int32, (rows, LANES), 1) - (LANES - BLK)
    t = lax.broadcasted_iota(jnp.int32, (rows, LANES), 0) % BLK

    def stores(turn):
        blocks = pl.ds(2 * turn, 2)
        return [
            pltpu.make_async_copy(acc_ref.at[blocks], acc_out.at[blocks], turn_sem.at[turn, 0]),
            pltpu.make_async_copy(lse_ref.at[blocks], lse_out.at[blocks], turn_sem.at[turn, 1]),
        ]

    def two_blocks(turn, carry):
        m, pair = turn // n_pairs, turn % n_pairs
        base = 2 * pair
        if n_src == 2:
            per = n_blk // 2
            base = jnp.where(pair < per, core, 1 - core) * n_blk + 2 * (pair % per)
        q_rows = q_ref.at[pl.ds(pl.multiple_of(2 * turn * BLK, 2 * BLK), 2 * BLK)]
        even = pl.ds(pl.multiple_of(base * BLK, LANES), span)

        def scores_of(n):
            q = with_selector(head_rows(q_rows, n, group), base + n, group)
            return jnp.dot(q, kaug[m, n, :, even], preferred_element_type=jnp.float32)

        def softmax_of(n, scores):
            parts = tiles(scores)
            parts[-1] = jnp.where(u > t, NEG, parts[-1])
            top = row_top(parts)
            return top, exponents(parts, top)

        def finish(n, top, weights):
            at = pl.ds(pl.multiple_of((base + n) * BLK, BLK), span)
            total = jnp.dot(weights, vaug[m, at, :], preferred_element_type=jnp.float32)
            acc_ref[2 * turn + n] = total[:, :HEAD_SIZE] / total[:, HEAD_SIZE:]
            lse_ref[2 * turn + n] = top + jnp.log(total[:, HEAD_SIZE:]) * LOG_SCALE

        in_pipeline(2, scores_of, softmax_of, finish)
        start_all(stores(turn))
        return carry

    lax.fori_loop(0, n_mine * n_pairs, two_blocks, 0)
    for turn in range(n_mine * n_pairs):
        wait_all(stores(turn))


def window_part(pos, pieces, places, kvs, bias, queries, q_recv, n_kv, n_src, n_blk, group, n_win):
    n_mine = len(kvs)
    width = group * HEAD_SIZE
    rows = group * BLK
    n_rows = n_win * BLK
    n_turns = n_mine * n_src * n_blk // 2
    q_args = [queries] if n_src == 1 else [queries, q_recv]
    out_shape = jax.ShapeDtypeStruct((2 * n_turns, rows, LANES), jnp.float32)
    sizes = [piece.shape[0] for piece in pieces]
    keys = 2 * n_turns * rows * (SMAX + 1) * BLK
    return pl.pallas_call(
        functools.partial(window_kernel, sizes, places, kvs, n_kv, n_src, n_blk, group),
        in_specs=[pl.BlockSpec(memory_space=pltpu.SMEM)]
        + [ANY] * (len(pieces) + 1 + n_src),
        out_specs=[ANY, ANY],
        scratch_shapes=[
            pltpu.VMEM((n_mine, n_rows, 2 * HEAD_SIZE), jnp.bfloat16),
            pltpu.VMEM((n_mine,) + bias.shape[1:], jnp.bfloat16),
            pltpu.VMEM((n_mine, 2, 2 * LANES, n_rows - BLK), jnp.bfloat16),
            pltpu.VMEM((n_mine, n_rows, 2 * LANES), jnp.bfloat16),
            pltpu.VMEM((2 * n_turns * BLK, width), jnp.bfloat16),
            pltpu.VMEM(out_shape.shape, jnp.float32),
            pltpu.VMEM(out_shape.shape, jnp.float32),
            pltpu.SemaphoreType.DMA((n_mine * (len(pieces) + 1 + n_src),)),
            pltpu.SemaphoreType.DMA((n_turns, 2)),
        ],
        out_shape=[out_shape, out_shape],
        compiler_params=pltpu.CompilerParams(vmem_limit_bytes=VMEM_LIMIT),
        cost_estimate=pl.CostEstimate(
            flops=keys * 1024, bytes_accessed=16 * 1024 * 1024, transcendentals=keys
        ),
    )(pos, *pieces, bias, *q_args)


def vertical_kernel(sources, kvs, n_kv, n_vert, group, n_blk, n_src, n_dst, other, direct, pos_ref, *refs):
    n_pieces = max(source[0] for source in sources) + 1
    n_mine = len(kvs)
    pieces, refs = refs[:n_pieces], refs[n_pieces:]
    bias_ref, refs = refs[0], refs[1:]
    q_in, refs = refs[:n_src], refs[n_src:]
    states_in, refs = refs[:2], refs[2:]
    n_outs = 1 + n_mine * (n_src - 1) if direct else n_mine * n_src
    outs_ref, refs = refs[:n_outs], refs[n_outs:]
    table, mask, kaug, vaug, q_ref, acc_ref, lse_ref, out_ref, sem, turn_sem = refs
    core, tp_pos = pos_ref[0], pos_ref[1]
    per_dst = n_blk // n_dst
    n_keys = vaug.shape[1]
    n_mask = bias_ref.shape[1]
    group_rows = n_vert * PIECE
    used = (N_PIECES // 2) * group_rows
    width = group * HEAD_SIZE
    base = 0
    if n_dst > 1:
        base = (1 - tp_pos if other else tp_pos) * per_dst
    count = iter(range(sem.shape[0]))

    loads = []
    for m, j in enumerate(kvs):
        for index, (piece, part) in enumerate(sources):
            slot = pos_ref[2 + index]
            rows = pl.ds(pl.multiple_of((slot // 2) * group_rows, PIECE), group_rows)
            loads.append(
                pltpu.make_async_copy(
                    pieces[piece].at[part, j], table.at[m, slot % 2, rows], sem.at[next(count)]
                )
            )
        loads.append(pltpu.make_async_copy(bias_ref.at[j], mask.at[m], sem.at[next(count)]))
    q_rows = pl.ds(pl.multiple_of(base * BLK, BLK), per_dst * BLK)

    def turn_loads(m, source, turn):
        j = kvs[m]
        first = pl.multiple_of((core * n_kv + j) * width, width)
        q_lanes = [pl.ds(first, width), pl.ds(j * width, width)]
        blocks = pl.ds((j * n_src + source) * n_blk + base, per_dst)
        return [
            pltpu.make_async_copy(
                q_in[source].at[q_rows, q_lanes[source]], q_ref.at[turn], turn_sem.at[turn, 0]
            ),
            pltpu.make_async_copy(
                states_in[0].at[blocks], acc_ref.at[turn], turn_sem.at[turn, 1]
            ),
            pltpu.make_async_copy(
                states_in[1].at[blocks], lse_ref.at[turn], turn_sem.at[turn, 2]
            ),
        ]

    start_all(loads)
    for m in range(n_mine):
        for source in range(n_src):
            start_all(turn_loads(m, source, m * n_src + source))
    for m in range(n_mine):
        if used < n_keys:
            empty = jnp.zeros((n_keys - used, LANES), jnp.bfloat16)
            table[m, 0, used:] = empty
            table[m, 1, used:] = empty
        vaug[m, :, HEAD_SIZE:] = jnp.ones((n_keys, LANES), jnp.bfloat16)
        kaug[m, HEAD_SIZE + n_mask:, :] = jnp.zeros((LANES - n_mask, n_keys), jnp.bfloat16)
    wait_all(loads)
    for m in range(n_mine):
        kaug[m, :HEAD_SIZE, :] = table[m, 0].T
        kaug[m, HEAD_SIZE:HEAD_SIZE + n_mask, :] = spread_mask(
            mask[m], lambda key: key % group_rows // PIECE, n_keys
        )
        if used < n_keys:
            kaug[m, HEAD_SIZE:HEAD_SIZE + n_mask, used:] = jnp.full((n_mask, n_keys - used), NEG, jnp.bfloat16)
        vaug[m, :, :HEAD_SIZE] = table[m, 1]

    def one_turn(turn, carry):
        j = turn // n_src
        first_block = base
        if n_src == 2:
            first_block = base + jnp.where(turn % 2 == 0, core, 1 - core) * n_blk
        wait_all(turn_loads(0, 0, turn))

        def scores_of(n):
            q = with_selector(head_rows(q_ref.at[turn], n, group), first_block + n, group)
            return jnp.dot(q, kaug[j], preferred_element_type=jnp.float32)

        def softmax_of(n, scores):
            old = lse_ref[turn, n]
            parts = tiles(scores)
            top = jnp.maximum(old, row_top(parts))
            return jnp.exp2((old - top) * SCALE), exponents(parts, top)

        def finish(n, shrink, weights):
            total = jnp.dot(weights, vaug[j], preferred_element_type=jnp.float32)
            weighted = total[:, :HEAD_SIZE] + acc_ref[turn, n] * shrink
            out = (weighted / (total[:, HEAD_SIZE:] + shrink)).astype(jnp.bfloat16)
            for h in range(group):
                lanes = slice(h * HEAD_SIZE, (h + 1) * HEAD_SIZE)
                out_ref[turn, n * BLK:(n + 1) * BLK, lanes] = out[h * BLK:(h + 1) * BLK]

        in_pipeline(per_dst, scores_of, softmax_of, finish)
        return carry

    lax.fori_loop(0, n_mine * n_src, one_turn, 0)
    stores = []
    for m in range(n_mine):
        for source in range(n_src):
            turn = m * n_src + source
            if direct and source == 0:
                column = pl.multiple_of(((tp_pos * n_src + core) * n_kv + kvs[m]) * width, width)
                target = outs_ref[0].at[:, pl.ds(column, width)]
            elif direct:
                target = outs_ref[1 + m]
            else:
                target = outs_ref[turn]
            stores.append(pltpu.make_async_copy(out_ref.at[turn], target, turn_sem.at[turn, 3]))
    start_all(stores)
    wait_all(stores)


def vertical_part(
    pos, pieces, sources, kvs, bias, queries, q_recv, states,
    n_kv, n_src, n_dst, other, direct, n_blk, group, n_vert,
):
    n_mine = len(kvs)
    n_turns = n_mine * n_src
    width = group * HEAD_SIZE
    rows = group * BLK
    per_dst = n_blk // n_dst
    n_keys = round_up(n_vert * BLK, LANES)
    q_args = [queries] if n_src == 1 else [queries, q_recv]
    piece = jax.ShapeDtypeStruct((per_dst * BLK, width), jnp.bfloat16)
    out_shapes = [piece] * n_turns
    if direct:
        whole = (per_dst * BLK, width * n_kv * n_src * n_dst)
        out_shapes = [jax.ShapeDtypeStruct(whole, jnp.bfloat16)] + [piece] * (n_mine * (n_src - 1))
    keys = n_turns * per_dst * rows * n_keys
    args = [*pieces, bias, *q_args, *states]
    return pl.pallas_call(
        functools.partial(
            vertical_kernel, sources, kvs, n_kv, n_vert, group, n_blk, n_src, n_dst, other, direct
        ),
        in_specs=[pl.BlockSpec(memory_space=pltpu.SMEM)] + [ANY] * len(args),
        out_specs=[ANY] * len(out_shapes),
        scratch_shapes=[
            pltpu.VMEM((n_mine, 2, n_keys, LANES), jnp.bfloat16),
            pltpu.VMEM((n_mine,) + bias.shape[1:], jnp.bfloat16),
            pltpu.VMEM((n_mine, 2 * LANES, n_keys), jnp.bfloat16),
            pltpu.VMEM((n_mine, n_keys, 2 * LANES), jnp.bfloat16),
            pltpu.VMEM((n_turns, per_dst * BLK, width), jnp.bfloat16),
            pltpu.VMEM((n_turns, per_dst, rows, LANES), jnp.float32),
            pltpu.VMEM((n_turns, per_dst, rows, LANES), jnp.float32),
            pltpu.VMEM((n_turns, per_dst * BLK, width), jnp.bfloat16),
            pltpu.SemaphoreType.DMA((n_mine * (N_PIECES + 1),)),
            pltpu.SemaphoreType.DMA((n_turns, 4)),
        ],
        out_shape=out_shapes,
        compiler_params=pltpu.CompilerParams(vmem_limit_bytes=(16 + round_up(8 * n_keys // 768, 8)) * 1024 * 1024),
        cost_estimate=pl.CostEstimate(
            flops=keys * 1024, bytes_accessed=8 * 1024 * 1024, transcendentals=keys
        ),
    )(pos, *args)


def split_kernel(n_kv, core_ref, kv_ref, out_ref, other_ref, mine_ref):
    half = other_ref.shape[1]
    core = core_ref[0]
    other_ref[...] = kv_ref[:, pl.ds(pl.multiple_of((1 - core) * half, half), half)]
    mine_ref[...] = kv_ref[:, pl.ds(pl.multiple_of(core * half, half), half)]
    for side in range(2):
        for j in range(n_kv):
            for part in range(2):
                lanes = ((side * n_kv + j) * 2 + part) * LANES
                for block in range(kv_ref.shape[0] // BLK):
                    for rg in range(BLK // PIECE):
                        at = block * BLK + rg * PIECE
                        out_ref[(rg * 2 + part) * 2 + side, block * n_kv + j] = kv_ref[
                            at:at + PIECE, lanes:lanes + LANES
                        ]


def split_rows(core, kv_rows, n_kv):
    rows, width = kv_rows.shape
    pieces = (2 * N_PIECES, rows // BLK * n_kv, PIECE, LANES)
    return pl.pallas_call(
        functools.partial(split_kernel, n_kv),
        in_specs=[pl.BlockSpec(memory_space=pltpu.SMEM), pl.BlockSpec(memory_space=pltpu.VMEM)],
        out_specs=[pl.BlockSpec(memory_space=pltpu.VMEM)] * 3,
        out_shape=[
            jax.ShapeDtypeStruct(shape, kv_rows.dtype)
            for shape in (pieces, (rows, width // 2), (rows, width // 2))
        ],
        compiler_params=pltpu.CompilerParams(vmem_limit_bytes=ALL_VMEM),
    )(core[None], kv_rows)


def join_kernel(core_ref, mine_ref, theirs_ref, here_ref, tail_ref):
    rows = mine_ref.shape[0]
    core = core_ref[0]
    here_ref[pl.ds(pl.multiple_of(core * rows, rows), rows), :] = mine_ref[...]
    here_ref[pl.ds(pl.multiple_of((1 - core) * rows, rows), rows), :] = theirs_ref[...]
    tail_ref[...] = here_ref[2 * rows - tail_ref.shape[0]:, :]


def join_rows(core, mine, theirs, tail):
    rows, width = mine.shape
    return pl.pallas_call(
        join_kernel,
        in_specs=[pl.BlockSpec(memory_space=pltpu.SMEM)] + [pl.BlockSpec(memory_space=pltpu.VMEM)] * 2,
        out_specs=[pl.BlockSpec(memory_space=pltpu.VMEM)] * 2,
        out_shape=[jax.ShapeDtypeStruct((size, width), mine.dtype) for size in (2 * rows, tail)],
        compiler_params=pltpu.CompilerParams(vmem_limit_bytes=VMEM_LIMIT // 4),
    )(core[None], mine, theirs)


def select_kernel(n_kv, n_vert, index_ref, table, out):
    for j in range(n_kv):
        for unit in range(n_vert):
            rows = slice(unit * PIECE, (unit + 1) * PIECE)
            out[j, rows, :] = table[index_ref[j * n_vert + unit]]


def select_units(index, table, n_kv, n_vert):
    return pl.pallas_call(
        functools.partial(select_kernel, n_kv, n_vert),
        in_specs=[
            pl.BlockSpec(memory_space=pltpu.SMEM),
            pl.BlockSpec(memory_space=pltpu.VMEM),
        ],
        out_specs=pl.BlockSpec(memory_space=pltpu.VMEM),
        out_shape=jax.ShapeDtypeStruct((n_kv, n_vert * PIECE, LANES), jnp.bfloat16),
        compiler_params=pltpu.CompilerParams(vmem_limit_bytes=8 * 1024 * 1024),
    )(index, table)


def assemble_kernel(n, column_ref, *refs):
    pieces, (_, out), buffers, sem = refs[:n], refs[n:n + 2], refs[n + 2:-1], refs[-1]
    loads = [pltpu.make_async_copy(pieces[i], buffers[i], sem.at[0, i]) for i in range(n)]
    start_all(loads)
    stores = []
    for i in range(n):
        loads[i].wait()
        width = buffers[i].shape[1]
        start = pl.multiple_of(column_ref[i], width)
        stores.append(
            pltpu.make_async_copy(buffers[i], out.at[:, pl.ds(start, width)], sem.at[1, i])
        )
        stores[-1].start()
    wait_all(stores)


def assemble(out, results, vmem):
    pieces = [piece for piece, _ in results]
    columns = jnp.stack([column for _, column in results]).astype(jnp.int32)
    n = len(pieces)
    return pl.pallas_call(
        functools.partial(assemble_kernel, n),
        in_specs=[pl.BlockSpec(memory_space=pltpu.SMEM)] + [ANY] * (n + 1),
        out_specs=ANY,
        out_shape=jax.ShapeDtypeStruct(out.shape, out.dtype),
        scratch_shapes=[pltpu.VMEM(piece.shape, piece.dtype) for piece in pieces]
        + [pltpu.SemaphoreType.DMA((2, n))],
        input_output_aliases={n + 1: 0},
        compiler_params=pltpu.CompilerParams(vmem_limit_bytes=vmem),
    )(columns, *pieces, out)


def mask_tables(vert, slash, first, n_query, n_win, n_vert, n_blocks):
    n_kv, group = vert.shape[:2]
    blocks = jnp.arange(n_blocks, dtype=jnp.int32)
    present = jnp.any(vert.reshape(n_kv, -1)[:, :, None] == blocks, axis=1)
    before = blocks[None, :] < blocks[:, None]
    rank = jnp.sum((present[:, None, :] & before[None]).astype(jnp.int32), axis=2)
    unit = jnp.arange(n_vert, dtype=jnp.int32)
    chosen = present[:, None, :] & (rank[:, None, :] == unit[None, :, None])
    units = jnp.sum(jnp.where(chosen, blocks, 0), axis=2)

    def as_rows(live):
        bias = jnp.where(live, 0.0, NEG).astype(jnp.bfloat16)
        bias = bias.reshape(n_kv, n_query * group, live.shape[-1])
        return jnp.pad(bias, ((0, 0), (0, 0), (0, LANES - live.shape[-1])))

    query = first + jnp.arange(n_query, dtype=jnp.int32)
    window = first - SMAX + jnp.arange(n_win, dtype=jnp.int32)
    offset = query[:, None] - window[None, :]
    by_slash = jnp.any(offset[None, :, None, :, None] == slash[:, None, :, None, :], axis=4)
    by_vert = jnp.any(window[None, None, :, None] == vert[:, :, None, :], axis=3)
    near = (offset >= 0) & (offset <= SMAX) & (window >= 0)[None, :]
    live_w = near[None, :, None, :] & (by_slash | by_vert[:, None, :, :])
    listed = jnp.any(units[:, None, :, None] == vert[:, :, None, :], axis=3)
    far = query[None, :, None] - units[:, None, :] > SMAX
    live_v = far[:, :, None, :] & listed[:, None, :, :]
    return units, as_rows(live_w), as_rows(live_v)


def paired(queries, kv_rows, vertical, slash):
    n_seq = lax.axis_size("seq")
    n_chip = n_seq // 2
    n_far = n_chip // 2
    tok = queries.shape[0]
    n_blk = tok // BLK
    seq_pos, tp_pos = lax.axis_index("seq"), lax.axis_index("tp")
    core, chip = seq_pos % 2, seq_pos // 2
    near, far = chip % 2, chip // 2
    heads_loc = vertical.shape[0] // 2
    kv_loc = kv_rows.shape[1] // (2 * HEAD_SIZE)
    group = heads_loc // kv_loc
    n_kv = kv_loc // 2
    heads = n_kv * group
    n_blocks = n_seq * n_blk
    n_vert = vertical.shape[1] * 3 // 2 - 1
    n_query = 2 * n_blk
    n_win = n_query + SMAX
    kv_width = n_kv * 2 * HEAD_SIZE
    q_width = heads * HEAD_SIZE

    def by_chip(array, target):
        pairs = []
        for source in range(n_seq):
            to = target(source // 2)
            if to is not None:
                pairs.append((source, 2 * to + source % 2))
        return lax.ppermute(array, "seq", pairs)

    pair = [(i, i ^ 1) for i in range(n_seq)]
    split, kv_other, mine = split_rows(core, kv_rows, n_kv)
    theirs = lax.ppermute(kv_other, "seq", pair)

    held = lax.all_to_all(split, "seq", split_axis=0, concat_axis=0, tiled=True)
    held = held.reshape(n_blocks * n_kv, PIECE, LANES)

    extra = SMAX - n_query
    here, tail = join_rows(core, mine, theirs, extra * BLK)
    before = by_chip(here, lambda c: c + 1 if c + 1 < n_chip else None)
    back = by_chip(tail, lambda c: c + 2 if c + 2 < n_chip else None)

    q_rows, here, tail = lax.optimization_barrier((queries, here, tail))
    q_other = lax.dynamic_slice_in_dim(q_rows, (1 - core) * q_width, q_width, 1)
    from_pair = lax.ppermute(q_other, "seq", pair)

    first_head = tp_pos * heads_loc + core * heads
    my_vert = lax.dynamic_slice_in_dim(vertical, first_head, heads, 0).reshape(n_kv, group, -1)
    my_slash = lax.dynamic_slice_in_dim(slash, first_head, heads, 0).reshape(n_kv, group, -1)
    units, bias_w, bias_v = mask_tables(
        my_vert, my_slash, chip * n_query, n_query, n_win, n_vert, n_blocks
    )

    index = (units * n_kv + jnp.arange(n_kv, dtype=jnp.int32)[:, None]).reshape(-1)
    picked = select_units(index, held, n_kv, n_vert)
    picked, from_pair = lax.optimization_barrier((picked, from_pair))
    beside = by_chip(picked, lambda c: c ^ 1)
    both = jnp.where(near == 0, jnp.stack([picked, beside]), jnp.stack([beside, picked]))
    pieces, sources, slots = [both], [(0, 0), (0, 1)], [2 * far, 2 * far + 1]
    for step in range(1, n_far):
        pieces.append(by_chip(both, lambda c: (c + 2 * step) % n_chip))
        sources += [(step, 0), (step, 1)]
        owner = (far - step) % n_far
        slots += [2 * owner, 2 * owner + 1]

    pos = jnp.stack([core, tp_pos] + slots).astype(jnp.int32)
    states = window_part(
        pos, [here, back, before], [SMAX, 0, extra], tuple(range(n_kv)), bias_w, queries, from_pair,
        n_kv, 2, n_blk, group, n_win,
    )

    def swap(array, other_core, other_tp):
        pairs = []
        for source in range(n_seq):
            for t in range(2):
                pairs.append((source * 2 + t, (source ^ other_core) * 2 + (t ^ other_tp)))
        return lax.ppermute(array, ("seq", "tp"), pairs)

    results = []
    for other_tp, kvs in [(1, (j,)) for j in range(n_kv)] + [(0, tuple(range(n_kv)))]:
        outs = vertical_part(
            pos, pieces, sources, kvs, bias_v, queries, from_pair, states,
            n_kv, 2, 2, other_tp, not other_tp, n_blk, group, n_vert,
        )
        outs, states = lax.optimization_barrier((outs, states))
        from_tp = 1 - tp_pos if other_tp else tp_pos
        if not other_tp:
            out, *outs = outs
        cores = (0, 1) if other_tp else (1,)
        turns = [(j, other_core) for j in kvs for other_core in cores]
        for (j, other_core), piece in zip(turns, outs, strict=True):
            from_core = 1 - core if other_core else core
            column = ((from_tp * 2 + from_core) * n_kv + j) * group * HEAD_SIZE
            results.append((swap(piece, other_core, other_tp), column))
    early = 2 * (n_kv - 1)
    return assemble(assemble(out, results[:early], ALL_VMEM), results[early:], VMEM_LIMIT // 4)


def gathered(queries, kv_rows, vertical, slash):
    n_seq, n_tp = lax.axis_size("seq"), lax.axis_size("tp")
    tok = queries.shape[0]
    n_blk = tok // BLK
    seq_pos, tp_pos = lax.axis_index("seq"), lax.axis_index("tp")
    heads = vertical.shape[0] // n_tp
    n_kv = kv_rows.shape[1] // (2 * HEAD_SIZE)
    group = heads // n_kv
    n_blocks = n_seq * n_blk
    n_vert = vertical.shape[1] * 3 // 2 - 1
    n_win = n_blk + SMAX
    first = seq_pos * n_blk
    my_vert = lax.dynamic_slice_in_dim(vertical, tp_pos * heads, heads, 0)
    my_slash = lax.dynamic_slice_in_dim(slash, tp_pos * heads, heads, 0)
    units, bias_w, bias_v = mask_tables(
        my_vert.reshape(n_kv, group, -1), my_slash.reshape(n_kv, group, -1),
        first, n_blk, n_win, n_vert, n_blocks,
    )
    full = lax.all_gather(kv_rows, "seq", axis=0, tiled=True)
    padded = jnp.pad(full, ((SMAX * BLK, 0), (0, 0)))
    window = lax.dynamic_slice_in_dim(padded, first * BLK, n_win * BLK, 0)
    pos = jnp.stack([jnp.int32(0), tp_pos] + [jnp.int32(i) for i in range(N_PIECES)])
    states = window_part(
        pos, [window], [0], tuple(range(n_kv)), bias_w, queries, None, n_kv, 1, n_blk, group, n_win
    )
    blocks = full.reshape(n_blocks, BLK // PIECE, PIECE, n_kv, 2, LANES)
    listed = jnp.stack([blocks[units[j], :, :, j] for j in range(n_kv)])
    listed = jnp.transpose(listed, (2, 4, 0, 1, 3, 5))
    listed = listed.reshape(N_PIECES, n_kv, n_vert * PIECE, LANES)
    outs = vertical_part(
        pos, [listed], [(0, i) for i in range(N_PIECES)], tuple(range(n_kv)), bias_v, queries, None,
        states, n_kv, 1, 1, 0, True, n_blk, group, n_vert,
    )
    attended = outs[0]
    return lax.all_to_all(attended, "tp", split_axis=0, concat_axis=1, tiled=True)


def per_device(queries, kv_rows, vertical, slash):
    n_seq, n_tp = lax.axis_size("seq"), lax.axis_size("tp")
    kv_loc = kv_rows.shape[1] // (2 * HEAD_SIZE)
    n_blk = queries.shape[0] // BLK
    if n_seq == 2 * N_PIECES and n_tp == 2 and kv_loc % 2 == 0 and n_blk == 4:
        return paired(queries, kv_rows, vertical, slash)
    return gathered(queries, kv_rows, vertical, slash)


def solution(mesh):
    return jax.shard_map(
        per_device,
        mesh=mesh,
        in_specs=(P("seq", "tp"), P("seq", "tp"), P(), P()),
        out_specs=P(("seq", "tp"), None),
        check_vma=False,
    )
```

```python
import functools
import math

import jax
import jax.numpy as jnp
from jax import lax
from jax.experimental import pallas as pl
from jax.experimental.pallas import tpu as pltpu
from jax.sharding import PartitionSpec as P

HEAD_SIZE = 128
BLK = 64
SMAX = 11
PIECE = 16
N_PIECES = (BLK // PIECE) * 2
LANES = 128
NEG = -1e30
SCALE = math.log2(math.e) / math.sqrt(HEAD_SIZE)
LOG_SCALE = math.sqrt(HEAD_SIZE)
ANY = pl.BlockSpec(memory_space=pl.ANY)


VMEM_LIMIT = 32 * 1024 * 1024
ALL_VMEM = 60 * 1024 * 1024


def round_up(value, unit):
    return (value + unit - 1) // unit * unit


def head_rows(ref, block, group):
    rows = slice(block * BLK, (block + 1) * BLK)
    heads = [ref[rows, h * HEAD_SIZE:(h + 1) * HEAD_SIZE] for h in range(group)]
    return jnp.concatenate(heads, axis=0)


def with_selector(q, block, group):
    shape = (q.shape[0], LANES)
    wanted = lax.broadcasted_iota(jnp.int32, shape, 0) // BLK + block * group
    pick = lax.broadcasted_iota(jnp.int32, shape, 1) == wanted
    return jnp.concatenate([q, jnp.where(pick, 1.0, 0.0).astype(jnp.bfloat16)], axis=1)


def in_pipeline(count, scores_of, softmax_of, finish):
    scores = scores_of(0)
    waiting = None
    for n in range(count):
        following = scores_of(n + 1) if n + 1 < count else None
        current = softmax_of(n, scores)
        if waiting is not None:
            finish(*waiting)
        waiting = (n, *current)
        scores = following
    finish(*waiting)


def tiles(array):
    return [array[:, at:at + LANES] for at in range(0, array.shape[1], LANES)]


def row_top(parts):
    top = functools.reduce(jnp.maximum, parts)
    return jnp.broadcast_to(jnp.max(top, axis=1, keepdims=True), top.shape)


def exponents(parts, top):
    return jnp.concatenate(
        [jnp.exp2((part - top) * SCALE).astype(jnp.bfloat16) for part in parts], axis=1
    )


def start_all(copies):
    for copy in copies:
        copy.start()


def wait_all(copies):
    for copy in copies:
        copy.wait()


def spread_mask(table, block_of_key, n_keys):
    shape = (LANES, n_keys)
    key = lax.broadcasted_iota(jnp.int32, shape, 1)
    own = lax.broadcasted_iota(jnp.int32, shape, 0) == block_of_key(key)
    own = jnp.where(own, 1.0, 0.0).astype(jnp.bfloat16)
    return jnp.dot(table, own, preferred_element_type=jnp.float32).astype(jnp.bfloat16)


def window_kernel(sizes, places, kvs, n_kv, n_src, n_blk, group, pos_ref, *refs):
    n_mine = len(kvs)
    n_pieces = len(sizes)
    pieces, refs = refs[:n_pieces], refs[n_pieces:]
    bias_ref, refs = refs[0], refs[1:]
    q_in, refs = refs[:n_src], refs[n_src:]
    acc_out, lse_out, table, mask, kaug, vaug, q_ref, acc_ref, lse_ref, sem, turn_sem = refs
    core = pos_ref[0]
    n_rows = table.shape[1]
    n_lanes = kaug.shape[3]
    n_mask = bias_ref.shape[1]
    width = group * HEAD_SIZE
    span = (SMAX + 1) * BLK
    rows = group * BLK
    tok = n_blk * BLK
    n_pairs = n_src * n_blk // 2
    count = iter(range(sem.shape[0]))

    loads = []
    for m, j in enumerate(kvs):
        mine = []
        lanes = pl.ds(j * 2 * HEAD_SIZE, 2 * HEAD_SIZE)
        for index in range(n_pieces):
            at = pl.ds(places[index] * BLK, sizes[index])
            mine.append((pieces[index].at[:, lanes], table.at[m, at]))
        mine.append((bias_ref.at[j], mask.at[m]))
        first = pl.multiple_of((core * n_kv + j) * width, width)
        q_lanes = [pl.ds(first, width), pl.ds(j * width, width)]
        for source in range(n_src):
            at = pl.ds((m * n_src + source) * tok, tok)
            mine.append((q_in[source].at[:, q_lanes[source]], q_ref.at[at]))
        loads.append([pltpu.make_async_copy(*pair, sem.at[next(count)]) for pair in mine])
    for mine in loads:
        start_all(mine)
    for m in range(n_mine):
        vaug[m, :, HEAD_SIZE:] = jnp.ones((n_rows, LANES), jnp.bfloat16)
        for odd in range(2):
            kaug[m, odd, HEAD_SIZE + n_mask:, :] = jnp.zeros((LANES - n_mask, n_lanes), jnp.bfloat16)
    for m in range(n_mine):
        wait_all(loads[m])
        for odd in range(2):
            kaug[m, odd, :HEAD_SIZE, :] = table[m, odd * BLK:odd * BLK + n_lanes, :HEAD_SIZE].T
            kaug[m, odd, HEAD_SIZE:HEAD_SIZE + n_mask, :] = spread_mask(
                mask[m], lambda key: key // BLK + odd, n_lanes
            )
        vaug[m, :, :HEAD_SIZE] = table[m, :, HEAD_SIZE:]

    u = lax.broadcasted_iota(jnp.int32, (rows, LANES), 1) - (LANES - BLK)
    t = lax.broadcasted_iota(jnp.int32, (rows, LANES), 0) % BLK

    def stores(turn):
        blocks = pl.ds(2 * turn, 2)
        return [
            pltpu.make_async_copy(acc_ref.at[blocks], acc_out.at[blocks], turn_sem.at[turn, 0]),
            pltpu.make_async_copy(lse_ref.at[blocks], lse_out.at[blocks], turn_sem.at[turn, 1]),
        ]

    def two_blocks(turn, carry):
        m, pair = turn // n_pairs, turn % n_pairs
        base = 2 * pair
        if n_src == 2:
            per = n_blk // 2
            base = jnp.where(pair < per, core, 1 - core) * n_blk + 2 * (pair % per)
        q_rows = q_ref.at[pl.ds(pl.multiple_of(2 * turn * BLK, 2 * BLK), 2 * BLK)]
        even = pl.ds(pl.multiple_of(base * BLK, LANES), span)

        def scores_of(n):
            q = with_selector(head_rows(q_rows, n, group), base + n, group)
            return jnp.dot(q, kaug[m, n, :, even], preferred_element_type=jnp.float32)

        def softmax_of(n, scores):
            parts = tiles(scores)
            parts[-1] = jnp.where(u > t, NEG, parts[-1])
            top = row_top(parts)
            return top, exponents(parts, top)

        def finish(n, top, weights):
            at = pl.ds(pl.multiple_of((base + n) * BLK, BLK), span)
            total = jnp.dot(weights, vaug[m, at, :], preferred_element_type=jnp.float32)
            acc_ref[2 * turn + n] = total[:, :HEAD_SIZE] / total[:, HEAD_SIZE:]
            lse_ref[2 * turn + n] = top + jnp.log(total[:, HEAD_SIZE:]) * LOG_SCALE

        in_pipeline(2, scores_of, softmax_of, finish)
        start_all(stores(turn))
        return carry

    lax.fori_loop(0, n_mine * n_pairs, two_blocks, 0)
    for turn in range(n_mine * n_pairs):
        wait_all(stores(turn))


def window_part(pos, pieces, places, kvs, bias, queries, q_recv, n_kv, n_src, n_blk, group, n_win):
    n_mine = len(kvs)
    width = group * HEAD_SIZE
    rows = group * BLK
    n_rows = n_win * BLK
    n_turns = n_mine * n_src * n_blk // 2
    q_args = [queries] if n_src == 1 else [queries, q_recv]
    out_shape = jax.ShapeDtypeStruct((2 * n_turns, rows, LANES), jnp.float32)
    sizes = [piece.shape[0] for piece in pieces]
    keys = 2 * n_turns * rows * (SMAX + 1) * BLK
    return pl.pallas_call(
        functools.partial(window_kernel, sizes, places, kvs, n_kv, n_src, n_blk, group),
        in_specs=[pl.BlockSpec(memory_space=pltpu.SMEM)]
        + [ANY] * (len(pieces) + 1 + n_src),
        out_specs=[ANY, ANY],
        scratch_shapes=[
            pltpu.VMEM((n_mine, n_rows, 2 * HEAD_SIZE), jnp.bfloat16),
            pltpu.VMEM((n_mine,) + bias.shape[1:], jnp.bfloat16),
            pltpu.VMEM((n_mine, 2, 2 * LANES, n_rows - BLK), jnp.bfloat16),
            pltpu.VMEM((n_mine, n_rows, 2 * LANES), jnp.bfloat16),
            pltpu.VMEM((2 * n_turns * BLK, width), jnp.bfloat16),
            pltpu.VMEM(out_shape.shape, jnp.float32),
            pltpu.VMEM(out_shape.shape, jnp.float32),
            pltpu.SemaphoreType.DMA((n_mine * (len(pieces) + 1 + n_src),)),
            pltpu.SemaphoreType.DMA((n_turns, 2)),
        ],
        out_shape=[out_shape, out_shape],
        compiler_params=pltpu.CompilerParams(vmem_limit_bytes=VMEM_LIMIT),
        cost_estimate=pl.CostEstimate(
            flops=keys * 1024, bytes_accessed=16 * 1024 * 1024, transcendentals=keys
        ),
    )(pos, *pieces, bias, *q_args)


def vertical_kernel(sources, kvs, n_kv, n_vert, group, n_blk, n_src, n_dst, other, direct, pos_ref, *refs):
    n_pieces = max(source[0] for source in sources) + 1
    n_mine = len(kvs)
    pieces, refs = refs[:n_pieces], refs[n_pieces:]
    bias_ref, refs = refs[0], refs[1:]
    q_in, refs = refs[:n_src], refs[n_src:]
    states_in, refs = refs[:2], refs[2:]
    n_outs = 1 + n_mine * (n_src - 1) if direct else n_mine * n_src
    outs_ref, refs = refs[:n_outs], refs[n_outs:]
    table, mask, kaug, vaug, q_ref, acc_ref, lse_ref, out_ref, sem, turn_sem = refs
    core, tp_pos = pos_ref[0], pos_ref[1]
    per_dst = n_blk // n_dst
    n_keys = vaug.shape[1]
    n_mask = bias_ref.shape[1]
    group_rows = n_vert * PIECE
    used = (N_PIECES // 2) * group_rows
    width = group * HEAD_SIZE
    base = 0
    if n_dst > 1:
        base = (1 - tp_pos if other else tp_pos) * per_dst
    count = iter(range(sem.shape[0]))

    loads = []
    for m, j in enumerate(kvs):
        for index, (piece, part) in enumerate(sources):
            slot = pos_ref[2 + index]
            rows = pl.ds(pl.multiple_of((slot // 2) * group_rows, PIECE), group_rows)
            loads.append(
                pltpu.make_async_copy(
                    pieces[piece].at[part, j], table.at[m, slot % 2, rows], sem.at[next(count)]
                )
            )
        loads.append(pltpu.make_async_copy(bias_ref.at[j], mask.at[m], sem.at[next(count)]))
    q_rows = pl.ds(pl.multiple_of(base * BLK, BLK), per_dst * BLK)

    def turn_loads(m, source, turn):
        j = kvs[m]
        first = pl.multiple_of((core * n_kv + j) * width, width)
        q_lanes = [pl.ds(first, width), pl.ds(j * width, width)]
        blocks = pl.ds((j * n_src + source) * n_blk + base, per_dst)
        return [
            pltpu.make_async_copy(
                q_in[source].at[q_rows, q_lanes[source]], q_ref.at[turn], turn_sem.at[turn, 0]
            ),
            pltpu.make_async_copy(
                states_in[0].at[blocks], acc_ref.at[turn], turn_sem.at[turn, 1]
            ),
            pltpu.make_async_copy(
                states_in[1].at[blocks], lse_ref.at[turn], turn_sem.at[turn, 2]
            ),
        ]

    start_all(loads)
    for m in range(n_mine):
        for source in range(n_src):
            start_all(turn_loads(m, source, m * n_src + source))
    for m in range(n_mine):
        if used < n_keys:
            empty = jnp.zeros((n_keys - used, LANES), jnp.bfloat16)
            table[m, 0, used:] = empty
            table[m, 1, used:] = empty
        vaug[m, :, HEAD_SIZE:] = jnp.ones((n_keys, LANES), jnp.bfloat16)
        kaug[m, HEAD_SIZE + n_mask:, :] = jnp.zeros((LANES - n_mask, n_keys), jnp.bfloat16)
    wait_all(loads)
    for m in range(n_mine):
        kaug[m, :HEAD_SIZE, :] = table[m, 0].T
        kaug[m, HEAD_SIZE:HEAD_SIZE + n_mask, :] = spread_mask(
            mask[m], lambda key: key % group_rows // PIECE, n_keys
        )
        if used < n_keys:
            kaug[m, HEAD_SIZE:HEAD_SIZE + n_mask, used:] = jnp.full((n_mask, n_keys - used), NEG, jnp.bfloat16)
        vaug[m, :, :HEAD_SIZE] = table[m, 1]

    def one_turn(turn, carry):
        j = turn // n_src
        first_block = base
        if n_src == 2:
            first_block = base + jnp.where(turn % 2 == 0, core, 1 - core) * n_blk
        wait_all(turn_loads(0, 0, turn))

        def scores_of(n):
            q = with_selector(head_rows(q_ref.at[turn], n, group), first_block + n, group)
            return jnp.dot(q, kaug[j], preferred_element_type=jnp.float32)

        def softmax_of(n, scores):
            old = lse_ref[turn, n]
            parts = tiles(scores)
            top = jnp.maximum(old, row_top(parts))
            return jnp.exp2((old - top) * SCALE), exponents(parts, top)

        def finish(n, shrink, weights):
            total = jnp.dot(weights, vaug[j], preferred_element_type=jnp.float32)
            weighted = total[:, :HEAD_SIZE] + acc_ref[turn, n] * shrink
            out = (weighted / (total[:, HEAD_SIZE:] + shrink)).astype(jnp.bfloat16)
            for h in range(group):
                lanes = slice(h * HEAD_SIZE, (h + 1) * HEAD_SIZE)
                out_ref[turn, n * BLK:(n + 1) * BLK, lanes] = out[h * BLK:(h + 1) * BLK]

        in_pipeline(per_dst, scores_of, softmax_of, finish)
        return carry

    lax.fori_loop(0, n_mine * n_src, one_turn, 0)
    stores = []
    for m in range(n_mine):
        for source in range(n_src):
            turn = m * n_src + source
            if direct and source == 0:
                column = pl.multiple_of(((tp_pos * n_src + core) * n_kv + kvs[m]) * width, width)
                target = outs_ref[0].at[:, pl.ds(column, width)]
            elif direct:
                target = outs_ref[1 + m]
            else:
                target = outs_ref[turn]
            stores.append(pltpu.make_async_copy(out_ref.at[turn], target, turn_sem.at[turn, 3]))
    start_all(stores)
    wait_all(stores)


def vertical_part(
    pos, pieces, sources, kvs, bias, queries, q_recv, states,
    n_kv, n_src, n_dst, other, direct, n_blk, group, n_vert,
):
    n_mine = len(kvs)
    n_turns = n_mine * n_src
    width = group * HEAD_SIZE
    rows = group * BLK
    per_dst = n_blk // n_dst
    n_keys = round_up(n_vert * BLK, LANES)
    q_args = [queries] if n_src == 1 else [queries, q_recv]
    piece = jax.ShapeDtypeStruct((per_dst * BLK, width), jnp.bfloat16)
    out_shapes = [piece] * n_turns
    if direct:
        whole = (per_dst * BLK, width * n_kv * n_src * n_dst)
        out_shapes = [jax.ShapeDtypeStruct(whole, jnp.bfloat16)] + [piece] * (n_mine * (n_src - 1))
    keys = n_turns * per_dst * rows * n_keys
    args = [*pieces, bias, *q_args, *states]
    return pl.pallas_call(
        functools.partial(
            vertical_kernel, sources, kvs, n_kv, n_vert, group, n_blk, n_src, n_dst, other, direct
        ),
        in_specs=[pl.BlockSpec(memory_space=pltpu.SMEM)] + [ANY] * len(args),
        out_specs=[ANY] * len(out_shapes),
        scratch_shapes=[
            pltpu.VMEM((n_mine, 2, n_keys, LANES), jnp.bfloat16),
            pltpu.VMEM((n_mine,) + bias.shape[1:], jnp.bfloat16),
            pltpu.VMEM((n_mine, 2 * LANES, n_keys), jnp.bfloat16),
            pltpu.VMEM((n_mine, n_keys, 2 * LANES), jnp.bfloat16),
            pltpu.VMEM((n_turns, per_dst * BLK, width), jnp.bfloat16),
            pltpu.VMEM((n_turns, per_dst, rows, LANES), jnp.float32),
            pltpu.VMEM((n_turns, per_dst, rows, LANES), jnp.float32),
            pltpu.VMEM((n_turns, per_dst * BLK, width), jnp.bfloat16),
            pltpu.SemaphoreType.DMA((n_mine * (N_PIECES + 1),)),
            pltpu.SemaphoreType.DMA((n_turns, 4)),
        ],
        out_shape=out_shapes,
        compiler_params=pltpu.CompilerParams(vmem_limit_bytes=(16 + round_up(8 * n_keys // 768, 8)) * 1024 * 1024),
        cost_estimate=pl.CostEstimate(
            flops=keys * 1024, bytes_accessed=8 * 1024 * 1024, transcendentals=keys
        ),
    )(pos, *args)


def split_kernel(n_kv, core_ref, kv_ref, out_ref, other_ref, mine_ref):
    half = other_ref.shape[1]
    core = core_ref[0]
    other_ref[...] = kv_ref[:, pl.ds(pl.multiple_of((1 - core) * half, half), half)]
    mine_ref[...] = kv_ref[:, pl.ds(pl.multiple_of(core * half, half), half)]
    for side in range(2):
        for j in range(n_kv):
            for part in range(2):
                lanes = ((side * n_kv + j) * 2 + part) * LANES
                for block in range(kv_ref.shape[0] // BLK):
                    for rg in range(BLK // PIECE):
                        at = block * BLK + rg * PIECE
                        out_ref[(rg * 2 + part) * 2 + side, block * n_kv + j] = kv_ref[
                            at:at + PIECE, lanes:lanes + LANES
                        ]


def split_rows(core, kv_rows, n_kv):
    rows, width = kv_rows.shape
    pieces = (2 * N_PIECES, rows // BLK * n_kv, PIECE, LANES)
    return pl.pallas_call(
        functools.partial(split_kernel, n_kv),
        in_specs=[pl.BlockSpec(memory_space=pltpu.SMEM), pl.BlockSpec(memory_space=pltpu.VMEM)],
        out_specs=[pl.BlockSpec(memory_space=pltpu.VMEM)] * 3,
        out_shape=[
            jax.ShapeDtypeStruct(shape, kv_rows.dtype)
            for shape in (pieces, (rows, width // 2), (rows, width // 2))
        ],
        compiler_params=pltpu.CompilerParams(vmem_limit_bytes=ALL_VMEM),
    )(core[None], kv_rows)


def join_kernel(core_ref, mine_ref, theirs_ref, here_ref, tail_ref):
    rows = mine_ref.shape[0]
    core = core_ref[0]
    here_ref[pl.ds(pl.multiple_of(core * rows, rows), rows), :] = mine_ref[...]
    here_ref[pl.ds(pl.multiple_of((1 - core) * rows, rows), rows), :] = theirs_ref[...]
    tail_ref[...] = here_ref[2 * rows - tail_ref.shape[0]:, :]


def join_rows(core, mine, theirs, tail):
    rows, width = mine.shape
    return pl.pallas_call(
        join_kernel,
        in_specs=[pl.BlockSpec(memory_space=pltpu.SMEM)] + [pl.BlockSpec(memory_space=pltpu.VMEM)] * 2,
        out_specs=[pl.BlockSpec(memory_space=pltpu.VMEM)] * 2,
        out_shape=[jax.ShapeDtypeStruct((size, width), mine.dtype) for size in (2 * rows, tail)],
        compiler_params=pltpu.CompilerParams(vmem_limit_bytes=VMEM_LIMIT // 4),
    )(core[None], mine, theirs)


def select_kernel(n_kv, n_vert, index_ref, table, out):
    for j in range(n_kv):
        for unit in range(n_vert):
            rows = slice(unit * PIECE, (unit + 1) * PIECE)
            out[j, rows, :] = table[index_ref[j * n_vert + unit]]


def select_units(index, table, n_kv, n_vert):
    return pl.pallas_call(
        functools.partial(select_kernel, n_kv, n_vert),
        in_specs=[
            pl.BlockSpec(memory_space=pltpu.SMEM),
            pl.BlockSpec(memory_space=pltpu.VMEM),
        ],
        out_specs=pl.BlockSpec(memory_space=pltpu.VMEM),
        out_shape=jax.ShapeDtypeStruct((n_kv, n_vert * PIECE, LANES), jnp.bfloat16),
        compiler_params=pltpu.CompilerParams(vmem_limit_bytes=8 * 1024 * 1024),
    )(index, table)


def assemble_kernel(n, column_ref, *refs):
    pieces, (_, out), sem = refs[:n], refs[n:n + 2], refs[-1]
    copies = []
    for i in range(n):
        width = pieces[i].shape[1]
        start = pl.multiple_of(column_ref[i], width)
        copies.append(pltpu.make_async_copy(pieces[i], out.at[:, pl.ds(start, width)], sem.at[i]))
    start_all(copies)
    wait_all(copies)


def assemble(out, results, vmem):
    pieces = [piece for piece, _ in results]
    columns = jnp.stack([column for _, column in results]).astype(jnp.int32)
    n = len(pieces)
    return pl.pallas_call(
        functools.partial(assemble_kernel, n),
        in_specs=[pl.BlockSpec(memory_space=pltpu.SMEM)]
        + [pl.BlockSpec(memory_space=pltpu.VMEM)] * n
        + [ANY],
        out_specs=ANY,
        out_shape=jax.ShapeDtypeStruct(out.shape, out.dtype),
        scratch_shapes=[pltpu.SemaphoreType.DMA((n,))],
        input_output_aliases={n + 1: 0},
        compiler_params=pltpu.CompilerParams(vmem_limit_bytes=vmem),
    )(columns, *pieces, out)


def mask_tables(vert, slash, first, n_query, n_win, n_vert, n_blocks):
    n_kv, group = vert.shape[:2]
    blocks = jnp.arange(n_blocks, dtype=jnp.int32)
    present = jnp.any(vert.reshape(n_kv, -1)[:, :, None] == blocks, axis=1)
    before = blocks[None, :] < blocks[:, None]
    rank = jnp.sum((present[:, None, :] & before[None]).astype(jnp.int32), axis=2)
    unit = jnp.arange(n_vert, dtype=jnp.int32)
    chosen = present[:, None, :] & (rank[:, None, :] == unit[None, :, None])
    units = jnp.sum(jnp.where(chosen, blocks, 0), axis=2)

    def as_rows(live):
        bias = jnp.where(live, 0.0, NEG).astype(jnp.bfloat16)
        bias = bias.reshape(n_kv, n_query * group, live.shape[-1])
        return jnp.pad(bias, ((0, 0), (0, 0), (0, LANES - live.shape[-1])))

    query = first + jnp.arange(n_query, dtype=jnp.int32)
    window = first - SMAX + jnp.arange(n_win, dtype=jnp.int32)
    offset = query[:, None] - window[None, :]
    by_slash = jnp.any(offset[None, :, None, :, None] == slash[:, None, :, None, :], axis=4)
    by_vert = jnp.any(window[None, None, :, None] == vert[:, :, None, :], axis=3)
    near = (offset >= 0) & (offset <= SMAX) & (window >= 0)[None, :]
    live_w = near[None, :, None, :] & (by_slash | by_vert[:, None, :, :])
    listed = jnp.any(units[:, None, :, None] == vert[:, :, None, :], axis=3)
    far = query[None, :, None] - units[:, None, :] > SMAX
    live_v = far[:, :, None, :] & listed[:, None, :, :]
    return units, as_rows(live_w), as_rows(live_v)


def paired(queries, kv_rows, vertical, slash):
    n_seq = lax.axis_size("seq")
    n_chip = n_seq // 2
    n_far = n_chip // 2
    tok = queries.shape[0]
    n_blk = tok // BLK
    seq_pos, tp_pos = lax.axis_index("seq"), lax.axis_index("tp")
    core, chip = seq_pos % 2, seq_pos // 2
    near, far = chip % 2, chip // 2
    heads_loc = vertical.shape[0] // 2
    kv_loc = kv_rows.shape[1] // (2 * HEAD_SIZE)
    group = heads_loc // kv_loc
    n_kv = kv_loc // 2
    heads = n_kv * group
    n_blocks = n_seq * n_blk
    n_vert = vertical.shape[1] * 3 // 2 - 1
    n_query = 2 * n_blk
    n_win = n_query + SMAX
    kv_width = n_kv * 2 * HEAD_SIZE
    q_width = heads * HEAD_SIZE

    def by_chip(array, target):
        pairs = []
        for source in range(n_seq):
            to = target(source // 2)
            if to is not None:
                pairs.append((source, 2 * to + source % 2))
        return lax.ppermute(array, "seq", pairs)

    pair = [(i, i ^ 1) for i in range(n_seq)]
    split, kv_other, mine = split_rows(core, kv_rows, n_kv)
    theirs = lax.ppermute(kv_other, "seq", pair)

    held = lax.all_to_all(split, "seq", split_axis=0, concat_axis=0, tiled=True)
    held = held.reshape(n_blocks * n_kv, PIECE, LANES)

    extra = SMAX - n_query
    here, tail = join_rows(core, mine, theirs, extra * BLK)
    before = by_chip(here, lambda c: c + 1 if c + 1 < n_chip else None)
    back = by_chip(tail, lambda c: c + 2 if c + 2 < n_chip else None)

    q_rows, here, tail = lax.optimization_barrier((queries, here, tail))
    q_other = lax.dynamic_slice_in_dim(q_rows, (1 - core) * q_width, q_width, 1)
    from_pair = lax.ppermute(q_other, "seq", pair)

    first_head = tp_pos * heads_loc + core * heads
    my_vert = lax.dynamic_slice_in_dim(vertical, first_head, heads, 0).reshape(n_kv, group, -1)
    my_slash = lax.dynamic_slice_in_dim(slash, first_head, heads, 0).reshape(n_kv, group, -1)
    units, bias_w, bias_v = mask_tables(
        my_vert, my_slash, chip * n_query, n_query, n_win, n_vert, n_blocks
    )

    index = (units * n_kv + jnp.arange(n_kv, dtype=jnp.int32)[:, None]).reshape(-1)
    picked = select_units(index, held, n_kv, n_vert)
    picked, from_pair = lax.optimization_barrier((picked, from_pair))
    beside = by_chip(picked, lambda c: c ^ 1)
    both = jnp.where(near == 0, jnp.stack([picked, beside]), jnp.stack([beside, picked]))
    pieces, sources, slots = [both], [(0, 0), (0, 1)], [2 * far, 2 * far + 1]
    for step in range(1, n_far):
        pieces.append(by_chip(both, lambda c: (c + 2 * step) % n_chip))
        sources += [(step, 0), (step, 1)]
        owner = (far - step) % n_far
        slots += [2 * owner, 2 * owner + 1]

    pos = jnp.stack([core, tp_pos] + slots).astype(jnp.int32)
    states = window_part(
        pos, [here, back, before], [SMAX, 0, extra], tuple(range(n_kv)), bias_w, queries, from_pair,
        n_kv, 2, n_blk, group, n_win,
    )

    def swap(array, other_core, other_tp):
        pairs = []
        for source in range(n_seq):
            for t in range(2):
                pairs.append((source * 2 + t, (source ^ other_core) * 2 + (t ^ other_tp)))
        return lax.ppermute(array, ("seq", "tp"), pairs)

    results = []
    for other_tp, kvs in [(1, (j,)) for j in range(n_kv)] + [(0, tuple(range(n_kv)))]:
        outs = vertical_part(
            pos, pieces, sources, kvs, bias_v, queries, from_pair, states,
            n_kv, 2, 2, other_tp, not other_tp, n_blk, group, n_vert,
        )
        outs, states = lax.optimization_barrier((outs, states))
        from_tp = 1 - tp_pos if other_tp else tp_pos
        if not other_tp:
            out, *outs = outs
        cores = (0, 1) if other_tp else (1,)
        turns = [(j, other_core) for j in kvs for other_core in cores]
        for (j, other_core), piece in zip(turns, outs, strict=True):
            from_core = 1 - core if other_core else core
            column = ((from_tp * 2 + from_core) * n_kv + j) * group * HEAD_SIZE
            results.append((swap(piece, other_core, other_tp), column))
    early = 2 * (n_kv - 1)
    return assemble(assemble(out, results[:early], ALL_VMEM), results[early:], VMEM_LIMIT // 4)


def gathered(queries, kv_rows, vertical, slash):
    n_seq, n_tp = lax.axis_size("seq"), lax.axis_size("tp")
    tok = queries.shape[0]
    n_blk = tok // BLK
    seq_pos, tp_pos = lax.axis_index("seq"), lax.axis_index("tp")
    heads = vertical.shape[0] // n_tp
    n_kv = kv_rows.shape[1] // (2 * HEAD_SIZE)
    group = heads // n_kv
    n_blocks = n_seq * n_blk
    n_vert = vertical.shape[1] * 3 // 2 - 1
    n_win = n_blk + SMAX
    first = seq_pos * n_blk
    my_vert = lax.dynamic_slice_in_dim(vertical, tp_pos * heads, heads, 0)
    my_slash = lax.dynamic_slice_in_dim(slash, tp_pos * heads, heads, 0)
    units, bias_w, bias_v = mask_tables(
        my_vert.reshape(n_kv, group, -1), my_slash.reshape(n_kv, group, -1),
        first, n_blk, n_win, n_vert, n_blocks,
    )
    full = lax.all_gather(kv_rows, "seq", axis=0, tiled=True)
    padded = jnp.pad(full, ((SMAX * BLK, 0), (0, 0)))
    window = lax.dynamic_slice_in_dim(padded, first * BLK, n_win * BLK, 0)
    pos = jnp.stack([jnp.int32(0), tp_pos] + [jnp.int32(i) for i in range(N_PIECES)])
    states = window_part(
        pos, [window], [0], tuple(range(n_kv)), bias_w, queries, None, n_kv, 1, n_blk, group, n_win
    )
    blocks = full.reshape(n_blocks, BLK // PIECE, PIECE, n_kv, 2, LANES)
    listed = jnp.stack([blocks[units[j], :, :, j] for j in range(n_kv)])
    listed = jnp.transpose(listed, (2, 4, 0, 1, 3, 5))
    listed = listed.reshape(N_PIECES, n_kv, n_vert * PIECE, LANES)
    outs = vertical_part(
        pos, [listed], [(0, i) for i in range(N_PIECES)], tuple(range(n_kv)), bias_v, queries, None,
        states, n_kv, 1, 1, 0, True, n_blk, group, n_vert,
    )
    attended = outs[0]
    return lax.all_to_all(attended, "tp", split_axis=0, concat_axis=1, tiled=True)


def per_device(queries, kv_rows, vertical, slash):
    n_seq, n_tp = lax.axis_size("seq"), lax.axis_size("tp")
    kv_loc = kv_rows.shape[1] // (2 * HEAD_SIZE)
    n_blk = queries.shape[0] // BLK
    if n_seq == 2 * N_PIECES and n_tp == 2 and kv_loc % 2 == 0 and n_blk == 4:
        return paired(queries, kv_rows, vertical, slash)
    return gathered(queries, kv_rows, vertical, slash)


def solution(mesh):
    return jax.shard_map(
        per_device,
        mesh=mesh,
        in_specs=(P("seq", "tp"), P("seq", "tp"), P(), P()),
        out_specs=P(("seq", "tp"), None),
        check_vma=False,
    )
```

```python
import functools
import math

import jax
import jax.numpy as jnp
from jax import lax
from jax.experimental import pallas as pl
from jax.experimental.pallas import tpu as pltpu
from jax.sharding import PartitionSpec as P

HEAD_SIZE = 128
BLK = 64
SMAX = 11
PIECE = 16
N_PIECES = (BLK // PIECE) * 2
LANES = 128
NEG = -1e30
SCALE = math.log2(math.e) / math.sqrt(HEAD_SIZE)
LOG_SCALE = math.sqrt(HEAD_SIZE)
ANY = pl.BlockSpec(memory_space=pl.ANY)


VMEM_LIMIT = 32 * 1024 * 1024
ALL_VMEM = 60 * 1024 * 1024


def round_up(value, unit):
    return (value + unit - 1) // unit * unit


def head_rows(ref, block, group):
    rows = slice(block * BLK, (block + 1) * BLK)
    heads = [ref[rows, h * HEAD_SIZE:(h + 1) * HEAD_SIZE] for h in range(group)]
    return jnp.concatenate(heads, axis=0)


def with_selector(q, block, group):
    shape = (q.shape[0], LANES)
    wanted = lax.broadcasted_iota(jnp.int32, shape, 0) // BLK + block * group
    pick = lax.broadcasted_iota(jnp.int32, shape, 1) == wanted
    return jnp.concatenate([q, jnp.where(pick, 1.0, 0.0).astype(jnp.bfloat16)], axis=1)


def in_pipeline(count, scores_of, softmax_of, finish):
    scores = scores_of(0)
    waiting = None
    for n in range(count):
        following = scores_of(n + 1) if n + 1 < count else None
        current = softmax_of(n, scores)
        if waiting is not None:
            finish(*waiting)
        waiting = (n, *current)
        scores = following
    finish(*waiting)


def tiles(array):
    return [array[:, at:at + LANES] for at in range(0, array.shape[1], LANES)]


def row_top(parts):
    top = functools.reduce(jnp.maximum, parts)
    return jnp.broadcast_to(jnp.max(top, axis=1, keepdims=True), top.shape)


def exponents(parts, top):
    return jnp.concatenate(
        [jnp.exp2((part - top) * SCALE).astype(jnp.bfloat16) for part in parts], axis=1
    )


def start_all(copies):
    for copy in copies:
        copy.start()


def wait_all(copies):
    for copy in copies:
        copy.wait()


def spread_mask(table, block_of_key, n_keys):
    shape = (LANES, n_keys)
    key = lax.broadcasted_iota(jnp.int32, shape, 1)
    own = lax.broadcasted_iota(jnp.int32, shape, 0) == block_of_key(key)
    own = jnp.where(own, 1.0, 0.0).astype(jnp.bfloat16)
    return jnp.dot(table, own, preferred_element_type=jnp.float32).astype(jnp.bfloat16)


def window_kernel(sizes, places, kvs, n_kv, n_src, n_blk, group, pos_ref, *refs):
    n_mine = len(kvs)
    n_pieces = len(sizes)
    pieces, refs = refs[:n_pieces], refs[n_pieces:]
    bias_ref, refs = refs[0], refs[1:]
    q_in, refs = refs[:n_src], refs[n_src:]
    acc_out, lse_out, table, mask, kaug, vaug, q_ref, acc_ref, lse_ref, sem, turn_sem = refs
    core = pos_ref[0]
    n_rows = table.shape[1]
    n_lanes = kaug.shape[3]
    n_mask = bias_ref.shape[1]
    width = group * HEAD_SIZE
    span = (SMAX + 1) * BLK
    rows = group * BLK
    tok = n_blk * BLK
    n_pairs = n_src * n_blk // 2
    count = iter(range(sem.shape[0]))

    loads = []
    for m, j in enumerate(kvs):
        mine = []
        lanes = pl.ds(j * 2 * HEAD_SIZE, 2 * HEAD_SIZE)
        for index in range(n_pieces):
            at = pl.ds(places[index] * BLK, sizes[index])
            mine.append((pieces[index].at[:, lanes], table.at[m, at]))
        mine.append((bias_ref.at[j], mask.at[m]))
        first = pl.multiple_of((core * n_kv + j) * width, width)
        q_lanes = [pl.ds(first, width), pl.ds(j * width, width)]
        for source in range(n_src):
            at = pl.ds((m * n_src + source) * tok, tok)
            mine.append((q_in[source].at[:, q_lanes[source]], q_ref.at[at]))
        loads.append([pltpu.make_async_copy(*pair, sem.at[next(count)]) for pair in mine])
    for mine in loads:
        start_all(mine)
    for m in range(n_mine):
        vaug[m, :, HEAD_SIZE:] = jnp.ones((n_rows, LANES), jnp.bfloat16)
        for odd in range(2):
            kaug[m, odd, HEAD_SIZE + n_mask:, :] = jnp.zeros((LANES - n_mask, n_lanes), jnp.bfloat16)
    for m in range(n_mine):
        wait_all(loads[m])
        for odd in range(2):
            kaug[m, odd, :HEAD_SIZE, :] = table[m, odd * BLK:odd * BLK + n_lanes, :HEAD_SIZE].T
            kaug[m, odd, HEAD_SIZE:HEAD_SIZE + n_mask, :] = spread_mask(
                mask[m], lambda key: key // BLK + odd, n_lanes
            )
        vaug[m, :, :HEAD_SIZE] = table[m, :, HEAD_SIZE:]

    u = lax.broadcasted_iota(jnp.int32, (rows, LANES), 1) - (LANES - BLK)
    t = lax.broadcasted_iota(jnp.int32, (rows, LANES), 0) % BLK

    def stores(turn):
        blocks = pl.ds(2 * turn, 2)
        return [
            pltpu.make_async_copy(acc_ref.at[blocks], acc_out.at[blocks], turn_sem.at[turn, 0]),
            pltpu.make_async_copy(lse_ref.at[blocks], lse_out.at[blocks], turn_sem.at[turn, 1]),
        ]

    def two_blocks(turn, carry):
        m, pair = turn // n_pairs, turn % n_pairs
        base = 2 * pair
        if n_src == 2:
            per = n_blk // 2
            base = jnp.where(pair < per, core, 1 - core) * n_blk + 2 * (pair % per)
        q_rows = q_ref.at[pl.ds(pl.multiple_of(2 * turn * BLK, 2 * BLK), 2 * BLK)]
        even = pl.ds(pl.multiple_of(base * BLK, LANES), span)

        def scores_of(n):
            q = with_selector(head_rows(q_rows, n, group), base + n, group)
            return jnp.dot(q, kaug[m, n, :, even], preferred_element_type=jnp.float32)

        def softmax_of(n, scores):
            parts = tiles(scores)
            parts[-1] = jnp.where(u > t, NEG, parts[-1])
            top = row_top(parts)
            return top, exponents(parts, top)

        def finish(n, top, weights):
            at = pl.ds(pl.multiple_of((base + n) * BLK, BLK), span)
            total = jnp.dot(weights, vaug[m, at, :], preferred_element_type=jnp.float32)
            acc_ref[2 * turn + n] = total[:, :HEAD_SIZE] / total[:, HEAD_SIZE:]
            lse_ref[2 * turn + n] = top + jnp.log(total[:, HEAD_SIZE:]) * LOG_SCALE

        in_pipeline(2, scores_of, softmax_of, finish)
        start_all(stores(turn))
        return carry

    lax.fori_loop(0, n_mine * n_pairs, two_blocks, 0)
    for turn in range(n_mine * n_pairs):
        wait_all(stores(turn))


def window_part(pos, pieces, places, kvs, bias, queries, q_recv, n_kv, n_src, n_blk, group, n_win):
    n_mine = len(kvs)
    width = group * HEAD_SIZE
    rows = group * BLK
    n_rows = n_win * BLK
    n_turns = n_mine * n_src * n_blk // 2
    q_args = [queries] if n_src == 1 else [queries, q_recv]
    out_shape = jax.ShapeDtypeStruct((2 * n_turns, rows, LANES), jnp.float32)
    sizes = [piece.shape[0] for piece in pieces]
    keys = 2 * n_turns * rows * (SMAX + 1) * BLK
    return pl.pallas_call(
        functools.partial(window_kernel, sizes, places, kvs, n_kv, n_src, n_blk, group),
        in_specs=[pl.BlockSpec(memory_space=pltpu.SMEM)]
        + [ANY] * (len(pieces) + 1 + n_src),
        out_specs=[ANY, ANY],
        scratch_shapes=[
            pltpu.VMEM((n_mine, n_rows, 2 * HEAD_SIZE), jnp.bfloat16),
            pltpu.VMEM((n_mine,) + bias.shape[1:], jnp.bfloat16),
            pltpu.VMEM((n_mine, 2, 2 * LANES, n_rows - BLK), jnp.bfloat16),
            pltpu.VMEM((n_mine, n_rows, 2 * LANES), jnp.bfloat16),
            pltpu.VMEM((2 * n_turns * BLK, width), jnp.bfloat16),
            pltpu.VMEM(out_shape.shape, jnp.float32),
            pltpu.VMEM(out_shape.shape, jnp.float32),
            pltpu.SemaphoreType.DMA((n_mine * (len(pieces) + 1 + n_src),)),
            pltpu.SemaphoreType.DMA((n_turns, 2)),
        ],
        out_shape=[out_shape, out_shape],
        compiler_params=pltpu.CompilerParams(vmem_limit_bytes=VMEM_LIMIT),
        cost_estimate=pl.CostEstimate(
            flops=keys * 1024, bytes_accessed=16 * 1024 * 1024, transcendentals=keys
        ),
    )(pos, *pieces, bias, *q_args)


def vertical_kernel(sources, kvs, n_kv, n_vert, group, n_blk, n_src, n_dst, other, direct, pos_ref, *refs):
    n_pieces = max(source[0] for source in sources) + 1
    n_mine = len(kvs)
    pieces, refs = refs[:n_pieces], refs[n_pieces:]
    bias_ref, refs = refs[0], refs[1:]
    q_in, refs = refs[:n_src], refs[n_src:]
    states_in, refs = refs[:2], refs[2:]
    n_outs = 1 + n_mine * (n_src - 1) if direct else n_mine * n_src
    outs_ref, refs = refs[:n_outs], refs[n_outs:]
    table, mask, kaug, vaug, q_ref, acc_ref, lse_ref, out_ref, sem, turn_sem = refs
    core, tp_pos = pos_ref[0], pos_ref[1]
    per_dst = n_blk // n_dst
    n_keys = vaug.shape[1]
    n_mask = bias_ref.shape[1]
    group_rows = n_vert * PIECE
    used = (N_PIECES // 2) * group_rows
    width = group * HEAD_SIZE
    base = 0
    if n_dst > 1:
        base = (1 - tp_pos if other else tp_pos) * per_dst
    count = iter(range(sem.shape[0]))

    loads = []
    for m, j in enumerate(kvs):
        for index, (piece, part) in enumerate(sources):
            slot = pos_ref[2 + index]
            rows = pl.ds(pl.multiple_of((slot // 2) * group_rows, PIECE), group_rows)
            loads.append(
                pltpu.make_async_copy(
                    pieces[piece].at[part, j], table.at[m, slot % 2, rows], sem.at[next(count)]
                )
            )
        loads.append(pltpu.make_async_copy(bias_ref.at[j], mask.at[m], sem.at[next(count)]))
    q_rows = pl.ds(pl.multiple_of(base * BLK, BLK), per_dst * BLK)

    def turn_loads(m, source, turn):
        j = kvs[m]
        first = pl.multiple_of((core * n_kv + j) * width, width)
        q_lanes = [pl.ds(first, width), pl.ds(j * width, width)]
        blocks = pl.ds((j * n_src + source) * n_blk + base, per_dst)
        return [
            pltpu.make_async_copy(
                q_in[source].at[q_rows, q_lanes[source]], q_ref.at[turn], turn_sem.at[turn, 0]
            ),
            pltpu.make_async_copy(
                states_in[0].at[blocks], acc_ref.at[turn], turn_sem.at[turn, 1]
            ),
            pltpu.make_async_copy(
                states_in[1].at[blocks], lse_ref.at[turn], turn_sem.at[turn, 2]
            ),
        ]

    start_all(loads)
    for m in range(n_mine):
        for source in range(n_src):
            start_all(turn_loads(m, source, m * n_src + source))
    for m in range(n_mine):
        if used < n_keys:
            empty = jnp.zeros((n_keys - used, LANES), jnp.bfloat16)
            table[m, 0, used:] = empty
            table[m, 1, used:] = empty
        vaug[m, :, HEAD_SIZE:] = jnp.ones((n_keys, LANES), jnp.bfloat16)
        kaug[m, HEAD_SIZE + n_mask:, :] = jnp.zeros((LANES - n_mask, n_keys), jnp.bfloat16)
    wait_all(loads)
    for m in range(n_mine):
        kaug[m, :HEAD_SIZE, :] = table[m, 0].T
        kaug[m, HEAD_SIZE:HEAD_SIZE + n_mask, :] = spread_mask(
            mask[m], lambda key: key % group_rows // PIECE, n_keys
        )
        if used < n_keys:
            kaug[m, HEAD_SIZE:HEAD_SIZE + n_mask, used:] = jnp.full((n_mask, n_keys - used), NEG, jnp.bfloat16)
        vaug[m, :, :HEAD_SIZE] = table[m, 1]

    def one_turn(turn, carry):
        j = turn // n_src
        first_block = base
        if n_src == 2:
            first_block = base + jnp.where(turn % 2 == 0, core, 1 - core) * n_blk
        wait_all(turn_loads(0, 0, turn))

        def scores_of(n):
            q = with_selector(head_rows(q_ref.at[turn], n, group), first_block + n, group)
            return jnp.dot(q, kaug[j], preferred_element_type=jnp.float32)

        def softmax_of(n, scores):
            old = lse_ref[turn, n]
            parts = tiles(scores)
            top = jnp.maximum(old, row_top(parts))
            return jnp.exp2((old - top) * SCALE), exponents(parts, top)

        def finish(n, shrink, weights):
            total = jnp.dot(weights, vaug[j], preferred_element_type=jnp.float32)
            weighted = total[:, :HEAD_SIZE] + acc_ref[turn, n] * shrink
            out = (weighted / (total[:, HEAD_SIZE:] + shrink)).astype(jnp.bfloat16)
            for h in range(group):
                lanes = slice(h * HEAD_SIZE, (h + 1) * HEAD_SIZE)
                out_ref[turn, n * BLK:(n + 1) * BLK, lanes] = out[h * BLK:(h + 1) * BLK]

        in_pipeline(per_dst, scores_of, softmax_of, finish)
        return carry

    lax.fori_loop(0, n_mine * n_src, one_turn, 0)
    stores = []
    for m in range(n_mine):
        for source in range(n_src):
            turn = m * n_src + source
            if direct and source == 0:
                side = tp_pos * n_src + core if n_dst > 1 else 0
                column = pl.multiple_of((side * n_kv + kvs[m]) * width, width)
                target = outs_ref[0].at[:, pl.ds(column, width)]
            elif direct:
                target = outs_ref[1 + m]
            else:
                target = outs_ref[turn]
            stores.append(pltpu.make_async_copy(out_ref.at[turn], target, turn_sem.at[turn, 3]))
    start_all(stores)
    wait_all(stores)


def vertical_part(
    pos, pieces, sources, kvs, bias, queries, q_recv, states,
    n_kv, n_src, n_dst, other, direct, n_blk, group, n_vert,
):
    n_mine = len(kvs)
    n_turns = n_mine * n_src
    width = group * HEAD_SIZE
    rows = group * BLK
    per_dst = n_blk // n_dst
    n_keys = round_up(n_vert * BLK, LANES)
    q_args = [queries] if n_src == 1 else [queries, q_recv]
    piece = jax.ShapeDtypeStruct((per_dst * BLK, width), jnp.bfloat16)
    out_shapes = [piece] * n_turns
    if direct:
        whole = (per_dst * BLK, width * n_kv * n_src * n_dst)
        out_shapes = [jax.ShapeDtypeStruct(whole, jnp.bfloat16)] + [piece] * (n_mine * (n_src - 1))
    keys = n_turns * per_dst * rows * n_keys
    args = [*pieces, bias, *q_args, *states]
    return pl.pallas_call(
        functools.partial(
            vertical_kernel, sources, kvs, n_kv, n_vert, group, n_blk, n_src, n_dst, other, direct
        ),
        in_specs=[pl.BlockSpec(memory_space=pltpu.SMEM)] + [ANY] * len(args),
        out_specs=[ANY] * len(out_shapes),
        scratch_shapes=[
            pltpu.VMEM((n_mine, 2, n_keys, LANES), jnp.bfloat16),
            pltpu.VMEM((n_mine,) + bias.shape[1:], jnp.bfloat16),
            pltpu.VMEM((n_mine, 2 * LANES, n_keys), jnp.bfloat16),
            pltpu.VMEM((n_mine, n_keys, 2 * LANES), jnp.bfloat16),
            pltpu.VMEM((n_turns, per_dst * BLK, width), jnp.bfloat16),
            pltpu.VMEM((n_turns, per_dst, rows, LANES), jnp.float32),
            pltpu.VMEM((n_turns, per_dst, rows, LANES), jnp.float32),
            pltpu.VMEM((n_turns, per_dst * BLK, width), jnp.bfloat16),
            pltpu.SemaphoreType.DMA((n_mine * (N_PIECES + 1),)),
            pltpu.SemaphoreType.DMA((n_turns, 4)),
        ],
        out_shape=out_shapes,
        compiler_params=pltpu.CompilerParams(vmem_limit_bytes=(16 + round_up(8 * n_keys // 768, 8)) * 1024 * 1024),
        cost_estimate=pl.CostEstimate(
            flops=keys * 1024, bytes_accessed=8 * 1024 * 1024, transcendentals=keys
        ),
    )(pos, *args)


def split_kernel(n_kv, core_ref, kv_ref, out_ref, other_ref, mine_ref):
    half = other_ref.shape[1]
    core = core_ref[0]
    other_ref[...] = kv_ref[:, pl.ds(pl.multiple_of((1 - core) * half, half), half)]
    mine_ref[...] = kv_ref[:, pl.ds(pl.multiple_of(core * half, half), half)]
    for side in range(2):
        for j in range(n_kv):
            for part in range(2):
                lanes = ((side * n_kv + j) * 2 + part) * LANES
                for block in range(kv_ref.shape[0] // BLK):
                    for rg in range(BLK // PIECE):
                        at = block * BLK + rg * PIECE
                        out_ref[(rg * 2 + part) * 2 + side, block * n_kv + j] = kv_ref[
                            at:at + PIECE, lanes:lanes + LANES
                        ]


def split_rows(core, kv_rows, n_kv):
    rows, width = kv_rows.shape
    pieces = (2 * N_PIECES, rows // BLK * n_kv, PIECE, LANES)
    return pl.pallas_call(
        functools.partial(split_kernel, n_kv),
        in_specs=[pl.BlockSpec(memory_space=pltpu.SMEM), pl.BlockSpec(memory_space=pltpu.VMEM)],
        out_specs=[pl.BlockSpec(memory_space=pltpu.VMEM)] * 3,
        out_shape=[
            jax.ShapeDtypeStruct(shape, kv_rows.dtype)
            for shape in (pieces, (rows, width // 2), (rows, width // 2))
        ],
        compiler_params=pltpu.CompilerParams(vmem_limit_bytes=ALL_VMEM),
    )(core[None], kv_rows)


def join_kernel(core_ref, mine_ref, theirs_ref, here_ref, tail_ref):
    rows = mine_ref.shape[0]
    core = core_ref[0]
    here_ref[pl.ds(pl.multiple_of(core * rows, rows), rows), :] = mine_ref[...]
    here_ref[pl.ds(pl.multiple_of((1 - core) * rows, rows), rows), :] = theirs_ref[...]
    tail_ref[...] = here_ref[2 * rows - tail_ref.shape[0]:, :]


def join_rows(core, mine, theirs, tail):
    rows, width = mine.shape
    return pl.pallas_call(
        join_kernel,
        in_specs=[pl.BlockSpec(memory_space=pltpu.SMEM)] + [pl.BlockSpec(memory_space=pltpu.VMEM)] * 2,
        out_specs=[pl.BlockSpec(memory_space=pltpu.VMEM)] * 2,
        out_shape=[jax.ShapeDtypeStruct((size, width), mine.dtype) for size in (2 * rows, tail)],
        compiler_params=pltpu.CompilerParams(vmem_limit_bytes=VMEM_LIMIT // 4),
    )(core[None], mine, theirs)


def select_kernel(n_kv, n_vert, index_ref, table, out):
    for j in range(n_kv):
        for unit in range(n_vert):
            rows = slice(unit * PIECE, (unit + 1) * PIECE)
            out[j, rows, :] = table[index_ref[j * n_vert + unit]]


def select_units(index, table, n_kv, n_vert):
    return pl.pallas_call(
        functools.partial(select_kernel, n_kv, n_vert),
        in_specs=[
            pl.BlockSpec(memory_space=pltpu.SMEM),
            pl.BlockSpec(memory_space=pltpu.VMEM),
        ],
        out_specs=pl.BlockSpec(memory_space=pltpu.VMEM),
        out_shape=jax.ShapeDtypeStruct((n_kv, n_vert * PIECE, LANES), jnp.bfloat16),
        compiler_params=pltpu.CompilerParams(vmem_limit_bytes=8 * 1024 * 1024),
    )(index, table)


def assemble_kernel(n, column_ref, *refs):
    pieces, (_, out), sem = refs[:n], refs[n:n + 2], refs[-1]
    copies = []
    for i in range(n):
        width = pieces[i].shape[1]
        start = pl.multiple_of(column_ref[i], width)
        copies.append(pltpu.make_async_copy(pieces[i], out.at[:, pl.ds(start, width)], sem.at[i]))
    start_all(copies)
    wait_all(copies)


def assemble(out, results, vmem):
    pieces = [piece for piece, _ in results]
    columns = jnp.stack([column for _, column in results]).astype(jnp.int32)
    n = len(pieces)
    return pl.pallas_call(
        functools.partial(assemble_kernel, n),
        in_specs=[pl.BlockSpec(memory_space=pltpu.SMEM)]
        + [pl.BlockSpec(memory_space=pltpu.VMEM)] * n
        + [ANY],
        out_specs=ANY,
        out_shape=jax.ShapeDtypeStruct(out.shape, out.dtype),
        scratch_shapes=[pltpu.SemaphoreType.DMA((n,))],
        input_output_aliases={n + 1: 0},
        compiler_params=pltpu.CompilerParams(vmem_limit_bytes=vmem),
    )(columns, *pieces, out)


def mask_tables(vert, slash, first, n_query, n_win, n_vert, n_blocks):
    n_kv, group = vert.shape[:2]
    blocks = jnp.arange(n_blocks, dtype=jnp.int32)
    present = jnp.any(vert.reshape(n_kv, -1)[:, :, None] == blocks, axis=1)
    before = blocks[None, :] < blocks[:, None]
    rank = jnp.sum((present[:, None, :] & before[None]).astype(jnp.int32), axis=2)
    unit = jnp.arange(n_vert, dtype=jnp.int32)
    chosen = present[:, None, :] & (rank[:, None, :] == unit[None, :, None])
    units = jnp.sum(jnp.where(chosen, blocks, 0), axis=2)

    def as_rows(live):
        bias = jnp.where(live, 0.0, NEG).astype(jnp.bfloat16)
        bias = bias.reshape(n_kv, n_query * group, live.shape[-1])
        return jnp.pad(bias, ((0, 0), (0, 0), (0, LANES - live.shape[-1])))

    query = first + jnp.arange(n_query, dtype=jnp.int32)
    window = first - SMAX + jnp.arange(n_win, dtype=jnp.int32)
    offset = query[:, None] - window[None, :]
    by_slash = jnp.any(offset[None, :, None, :, None] == slash[:, None, :, None, :], axis=4)
    by_vert = jnp.any(window[None, None, :, None] == vert[:, :, None, :], axis=3)
    near = (offset >= 0) & (offset <= SMAX) & (window >= 0)[None, :]
    live_w = near[None, :, None, :] & (by_slash | by_vert[:, None, :, :])
    listed = jnp.any(units[:, None, :, None] == vert[:, :, None, :], axis=3)
    far = query[None, :, None] - units[:, None, :] > SMAX
    live_v = far[:, :, None, :] & listed[:, None, :, :]
    return units, as_rows(live_w), as_rows(live_v)


def paired(queries, kv_rows, vertical, slash):
    n_seq = lax.axis_size("seq")
    n_chip = n_seq // 2
    n_far = n_chip // 2
    tok = queries.shape[0]
    n_blk = tok // BLK
    seq_pos, tp_pos = lax.axis_index("seq"), lax.axis_index("tp")
    core, chip = seq_pos % 2, seq_pos // 2
    near, far = chip % 2, chip // 2
    heads_loc = vertical.shape[0] // 2
    kv_loc = kv_rows.shape[1] // (2 * HEAD_SIZE)
    group = heads_loc // kv_loc
    n_kv = kv_loc // 2
    heads = n_kv * group
    n_blocks = n_seq * n_blk
    n_vert = vertical.shape[1] * 3 // 2 - 1
    n_query = 2 * n_blk
    n_win = n_query + SMAX
    kv_width = n_kv * 2 * HEAD_SIZE
    q_width = heads * HEAD_SIZE

    def by_chip(array, target):
        pairs = []
        for source in range(n_seq):
            to = target(source // 2)
            if to is not None:
                pairs.append((source, 2 * to + source % 2))
        return lax.ppermute(array, "seq", pairs)

    pair = [(i, i ^ 1) for i in range(n_seq)]
    split, kv_other, mine = split_rows(core, kv_rows, n_kv)
    theirs = lax.ppermute(kv_other, "seq", pair)

    held = lax.all_to_all(split, "seq", split_axis=0, concat_axis=0, tiled=True)
    held = held.reshape(n_blocks * n_kv, PIECE, LANES)

    extra = SMAX - n_query
    here, tail = join_rows(core, mine, theirs, extra * BLK)
    before = by_chip(here, lambda c: c + 1 if c + 1 < n_chip else None)
    back = by_chip(tail, lambda c: c + 2 if c + 2 < n_chip else None)

    q_rows, here, tail = lax.optimization_barrier((queries, here, tail))
    q_other = lax.dynamic_slice_in_dim(q_rows, (1 - core) * q_width, q_width, 1)
    from_pair = lax.ppermute(q_other, "seq", pair)

    first_head = tp_pos * heads_loc + core * heads
    my_vert = lax.dynamic_slice_in_dim(vertical, first_head, heads, 0).reshape(n_kv, group, -1)
    my_slash = lax.dynamic_slice_in_dim(slash, first_head, heads, 0).reshape(n_kv, group, -1)
    units, bias_w, bias_v = mask_tables(
        my_vert, my_slash, chip * n_query, n_query, n_win, n_vert, n_blocks
    )

    index = (units * n_kv + jnp.arange(n_kv, dtype=jnp.int32)[:, None]).reshape(-1)
    picked = select_units(index, held, n_kv, n_vert)
    picked, from_pair = lax.optimization_barrier((picked, from_pair))
    beside = by_chip(picked, lambda c: c ^ 1)
    both = jnp.where(near == 0, jnp.stack([picked, beside]), jnp.stack([beside, picked]))
    pieces, sources, slots = [both], [(0, 0), (0, 1)], [2 * far, 2 * far + 1]
    for step in range(1, n_far):
        pieces.append(by_chip(both, lambda c: (c + 2 * step) % n_chip))
        sources += [(step, 0), (step, 1)]
        owner = (far - step) % n_far
        slots += [2 * owner, 2 * owner + 1]

    pos = jnp.stack([core, tp_pos] + slots).astype(jnp.int32)
    states = window_part(
        pos, [here, back, before], [SMAX, 0, extra], tuple(range(n_kv)), bias_w, queries, from_pair,
        n_kv, 2, n_blk, group, n_win,
    )

    def swap(array, other_core, other_tp):
        pairs = []
        for source in range(n_seq):
            for t in range(2):
                pairs.append((source * 2 + t, (source ^ other_core) * 2 + (t ^ other_tp)))
        return lax.ppermute(array, ("seq", "tp"), pairs)

    results = []
    for other_tp, kvs in [(1, (j,)) for j in range(n_kv)] + [(0, tuple(range(n_kv)))]:
        outs = vertical_part(
            pos, pieces, sources, kvs, bias_v, queries, from_pair, states,
            n_kv, 2, 2, other_tp, not other_tp, n_blk, group, n_vert,
        )
        outs, states = lax.optimization_barrier((outs, states))
        from_tp = 1 - tp_pos if other_tp else tp_pos
        if not other_tp:
            out, *outs = outs
        cores = (0, 1) if other_tp else (1,)
        turns = [(j, other_core) for j in kvs for other_core in cores]
        for (j, other_core), piece in zip(turns, outs, strict=True):
            from_core = 1 - core if other_core else core
            column = ((from_tp * 2 + from_core) * n_kv + j) * group * HEAD_SIZE
            results.append((swap(piece, other_core, other_tp), column))
    early = 2 * (n_kv - 1)
    return assemble(assemble(out, results[:early], ALL_VMEM), results[early:], VMEM_LIMIT // 4)


def gathered(queries, kv_rows, vertical, slash):
    n_seq, n_tp = lax.axis_size("seq"), lax.axis_size("tp")
    tok = queries.shape[0]
    n_blk = tok // BLK
    seq_pos, tp_pos = lax.axis_index("seq"), lax.axis_index("tp")
    heads = vertical.shape[0] // n_tp
    n_kv = kv_rows.shape[1] // (2 * HEAD_SIZE)
    group = heads // n_kv
    n_blocks = n_seq * n_blk
    n_vert = vertical.shape[1] * 3 // 2 - 1
    n_win = n_blk + SMAX
    first = seq_pos * n_blk
    my_vert = lax.dynamic_slice_in_dim(vertical, tp_pos * heads, heads, 0)
    my_slash = lax.dynamic_slice_in_dim(slash, tp_pos * heads, heads, 0)
    units, bias_w, bias_v = mask_tables(
        my_vert.reshape(n_kv, group, -1), my_slash.reshape(n_kv, group, -1),
        first, n_blk, n_win, n_vert, n_blocks,
    )
    full = lax.all_gather(kv_rows, "seq", axis=0, tiled=True)
    padded = jnp.pad(full, ((SMAX * BLK, 0), (0, 0)))
    window = lax.dynamic_slice_in_dim(padded, first * BLK, n_win * BLK, 0)
    pos = jnp.stack([jnp.int32(0), tp_pos] + [jnp.int32(i) for i in range(N_PIECES)])
    states = window_part(
        pos, [window], [0], tuple(range(n_kv)), bias_w, queries, None, n_kv, 1, n_blk, group, n_win
    )
    blocks = full.reshape(n_blocks, BLK // PIECE, PIECE, n_kv, 2, LANES)
    listed = jnp.stack([blocks[units[j], :, :, j] for j in range(n_kv)])
    listed = jnp.transpose(listed, (2, 4, 0, 1, 3, 5))
    listed = listed.reshape(N_PIECES, n_kv, n_vert * PIECE, LANES)
    outs = vertical_part(
        pos, [listed], [(0, i) for i in range(N_PIECES)], tuple(range(n_kv)), bias_v, queries, None,
        states, n_kv, 1, 1, 0, True, n_blk, group, n_vert,
    )
    attended = outs[0]
    return lax.all_to_all(attended, "tp", split_axis=0, concat_axis=1, tiled=True)


def per_device(queries, kv_rows, vertical, slash):
    n_seq, n_tp = lax.axis_size("seq"), lax.axis_size("tp")
    kv_loc = kv_rows.shape[1] // (2 * HEAD_SIZE)
    n_blk = queries.shape[0] // BLK
    if n_seq == 2 * N_PIECES and n_tp == 2 and kv_loc % 2 == 0 and n_blk == 4:
        return paired(queries, kv_rows, vertical, slash)
    return gathered(queries, kv_rows, vertical, slash)


def solution(mesh):
    return jax.shard_map(
        per_device,
        mesh=mesh,
        in_specs=(P("seq", "tp"), P("seq", "tp"), P(), P()),
        out_specs=P(("seq", "tp"), None),
        check_vma=False,
    )
```
